256 devices in a mesh: dp: 8 (over z), seq: 32 (over x, y, core).
Axes of the slice: x: 4, y: 4, z: 8, core: 2. Of those that a mesh axis runs over, the one named last changes fastest.
Arguments:
- queries: bfloat16 [8, 4096, 2048], P('dp', 'seq'), may hold values from -6 to 6
- keys: bfloat16 [8, 4096, 2048], P('dp', 'seq'), may hold values from -6 to 6
- values: bfloat16 [8, 4096, 2048], P('dp', 'seq'), may hold values from -6 to 6
- out_grad: bfloat16 [8, 4096, 2048], P('dp', 'seq'), may hold values from -6 to 6
- out_weight: bfloat16 [2048, 2048], P(('dp', 'seq')), may hold values from -0.125 to 0.125
Outputs:
- query_grad: bfloat16 [8, 4096, 2048], P('dp', 'seq')
- key_grad: bfloat16 [8, 4096, 2048], P('dp', 'seq')
- value_grad: bfloat16 [8, 4096, 2048], P('dp', 'seq')
- weight_grad: float32 [2048, 2048], P(('dp', 'seq'))
The draws below stay inside these ranges and needn't reach their ends.
All inputs are finite; a program needn't handle non-finite values.
Results may differ from the reference program's by a relative error of at most 0.011.
Values may be sent and summed in bfloat16 or wider, within the bound.
No kernel may reach another device: no remote copies, remote signals or barrier semaphores. Data moves between devices by JAX's collectives and lax.ppermute only.
A program may use at most 192 MiB of HBM per device.

```python
from functools import partial
import jax
import jax.numpy as jnp
from jax import lax

D = 2048
HEADS = 16
DH = 128
TOK_DEV = 128
HD = 2048
LENGTH = 4096
SEQS = 8


def steps_of(rng, dims, split, low, largest):
    gain, own = 1.0, jax.random.fold_in(rng, 6)
    for axis_at, blocks in split:
        steps = jnp.exp(jax.random.uniform(jax.random.fold_in(own, axis_at), (blocks,), jnp.float32, low / len(split), largest / len(split)))
        gain = gain * jnp.repeat(steps, dims[axis_at] // blocks).reshape([-1 if axis == axis_at else 1 for axis in range(len(dims))])
    return gain


def noise(own_key, extent, width, reach, cuts=(), kind=jnp.bfloat16):
    values = width * jax.random.normal(own_key, extent, jnp.float32)
    if cuts:
        values = values * steps_of(own_key, extent, cuts, -0.22, 0.18)
    return jnp.clip(values, -reach, reach).astype(kind)


def setup_inputs(seed: int = 0) -> dict:
    arg_keys = jax.random.split(jax.random.key(seed), 6)
    queries = noise(arg_keys[0], (SEQS, LENGTH, HD), 1.0, 6.0, ((0, 8), (1, 32)))
    keys = noise(arg_keys[1], (SEQS, LENGTH, HD), 1.0, 6.0, ((0, 8), (1, 32)))
    values = noise(arg_keys[2], (SEQS, LENGTH, HD), 1.0, 6.0, ((0, 8), (1, 32)))
    out_grad = noise(arg_keys[3], (SEQS, LENGTH, D), 1.0, 6.0, ((0, 8), (1, 32)))
    out_weight = noise(arg_keys[4], (HD, D), HD ** -0.5, 0.125, ((0, 256),))
    return {"queries": queries, "keys": keys, "values": values, "out_grad": out_grad, "out_weight": out_weight}


def feature(values_in):
    return jnp.where(values_in > 0, values_in + 1.0, jnp.exp(jnp.minimum(values_in, 0.0)))


def feature_slope(values_in):
    return jnp.where(values_in > 0, 1.0, jnp.exp(jnp.minimum(values_in, 0.0)))


def mix_sum(form, left, right):
    return jnp.einsum(form, left.astype(jnp.float32), right.astype(jnp.float32), precision=lax.Precision.HIGHEST)


def one_sequence(out_weight, arrays):
    queries, keys, values, out_grad = arrays
    blocks = LENGTH // TOK_DEV
    block_shape = (blocks, TOK_DEV, HEADS, DH)
    q_raw = queries.astype(jnp.float32).reshape(block_shape)
    k_raw = keys.astype(jnp.float32).reshape(block_shape)
    q_feat = feature(q_raw).astype(jnp.bfloat16)
    k_feat = feature(k_raw).astype(jnp.bfloat16)
    v_full = values.reshape(block_shape)
    positions = jnp.arange(TOK_DEV, dtype=jnp.int32)
    causal = (positions[:, None] >= positions[None, :]).astype(jnp.float32)
    zero_state = jnp.zeros((HEADS, DH, DH), jnp.float32)
    zero_norm = jnp.zeros((HEADS, DH), jnp.float32)

    def forward(carried, pieces):
        state_in, norm_in = carried
        q_b, k_b, v_b = pieces
        scores = mix_sum('thd,shd->hts', q_b, k_b) * causal
        scores_low = scores.astype(jnp.bfloat16)
        numer = mix_sum('hts,she->the', scores_low, v_b) + mix_sum('thd,hde->the', q_b, state_in)
        denoms = jnp.sum(scores, axis=2).T + mix_sum('thd,hd->th', q_b, norm_in)
        outputs = numer / denoms[:, :, None]
        updated = (state_in + mix_sum('shd,she->hde', k_b, v_b), norm_in + jnp.sum(k_b.astype(jnp.float32), axis=0))
        return updated, (outputs, denoms, state_in, norm_in)

    last, (outputs, denoms, states, norms) = lax.scan(forward, (zero_state, zero_norm), (q_feat, k_feat, v_full))
    attended = outputs.reshape(LENGTH, HD).astype(jnp.bfloat16)
    attn_grad = jnp.dot(out_grad, out_weight.T, preferred_element_type=jnp.float32).reshape(block_shape)
    scaled = attn_grad / denoms[:, :, :, None]
    residue = -jnp.sum(scaled * outputs, axis=3)

    def backward(carried, pieces):
        grad_state, grad_norm = carried
        q_b, k_b, v_b, g_b, r_b, st_in, nm_in = pieces
        g_low = g_b.astype(jnp.bfloat16)
        scores_low = (mix_sum('thd,shd->hts', q_b, k_b) * causal).astype(jnp.bfloat16)
        mixed_w = ((mix_sum('the,she->hts', g_low, v_b) + r_b.T[:, :, None]) * causal).astype(jnp.bfloat16)
        q_grad = mix_sum('hts,shd->thd', mixed_w, k_b) + mix_sum('the,hde->thd', g_b, st_in) + r_b[:, :, None] * nm_in[None]
        k_grad = mix_sum('hts,thd->shd', mixed_w, q_b) + mix_sum('hde,she->shd', grad_state, v_b) + grad_norm[None]
        v_grad = mix_sum('hts,the->she', scores_low, g_low) + mix_sum('hde,shd->she', grad_state, k_b)
        updated = (grad_state + mix_sum('thd,the->hde', q_b, g_b), grad_norm + mix_sum('th,thd->hd', r_b, q_b))
        return updated, (q_grad, k_grad, v_grad)

    last_back, (q_grad, k_grad, v_grad) = lax.scan(backward, (zero_state, zero_norm), (q_feat, k_feat, v_full, scaled, residue, states, norms), reverse=True)
    query_grad = (q_grad * feature_slope(q_raw)).reshape(LENGTH, HD).astype(jnp.bfloat16)
    key_grad = (k_grad * feature_slope(k_raw)).reshape(LENGTH, HD).astype(jnp.bfloat16)
    value_grad = v_grad.reshape(LENGTH, HD).astype(jnp.bfloat16)
    return attended, query_grad, key_grad, value_grad


def reference(queries, keys, values, out_grad, out_weight):
    attended, query_grad, key_grad, value_grad = lax.map(partial(one_sequence, out_weight), (queries, keys, values, out_grad))
    weight_grad = jnp.dot(attended.reshape(SEQS * LENGTH, HD).T, out_grad.reshape(SEQS * LENGTH, D), preferred_element_type=jnp.float32)
    return query_grad, key_grad, value_grad, weight_grad
```

```python
import functools

import jax
import jax.numpy as jnp
from jax import lax
from jax.experimental import pallas as pl
from jax.experimental.pallas import tpu as pltpu
from jax.sharding import Mesh, PartitionSpec as P

DH = 128
BLK = 128
BF = jnp.bfloat16
F32 = jnp.float32
NN = (((1,), (0,)), ((), ()))
NT = (((1,), (1,)), ((), ()))
TN = (((0,), (0,)), ((), ()))
HALF = DH // 2
ROWS = HALF + 8
PARAMS = pltpu.CompilerParams(vmem_limit_bytes=48 * 1024 * 1024)


def dot(left, right, dims):
    return lax.dot_general(left, right, dims, preferred_element_type=F32)


def split(wide):
    high = wide.astype(BF)
    return high, (wide - high.astype(F32)).astype(BF)


def feature(raw):
    return jnp.where(raw > 0, raw + 1.0, jnp.exp(jnp.minimum(raw, 0.0)))


def feature_slope(raw):
    return jnp.where(raw > 0, 1.0, jnp.exp(jnp.minimum(raw, 0.0)))


def features_of(raw):
    return feature(raw.astype(F32)).astype(BF)


def causal_mask():
    row = lax.broadcasted_iota(jnp.int32, (BLK, BLK), 0)
    col = lax.broadcasted_iota(jnp.int32, (BLK, BLK), 1)
    return row >= col


def state_of(ref):
    return jnp.concatenate([ref[0, :HALF], ref[1, :HALF]], axis=0), ref[0, HALF : HALF + 1]


def put_state(ref, matrix, vector):
    tail = jnp.broadcast_to(vector, (8, DH))
    for half in range(2):
        ref[half, :HALF] = matrix[half * HALF : (half + 1) * HALF]
        ref[half, HALF:] = tail


def call(body, grid, ins, outs, scratch=()):
    return pl.pallas_call(
        body,
        grid_spec=pltpu.PrefetchScalarGridSpec(
            num_scalar_prefetch=1,
            grid=grid,
            in_specs=[pl.BlockSpec(*spec) for spec in ins],
            out_specs=[pl.BlockSpec(spec[0], spec[1]) for spec in outs],
            scratch_shapes=list(scratch),
        ),
        out_shape=[jax.ShapeDtypeStruct(spec[2], spec[3]) for spec in outs],
        compiler_params=PARAMS,
    )


def pack_body(core, q_ref, k_ref, v_ref, out_ref):
    out_ref[0] = q_ref[...]
    out_ref[1] = k_ref[...]
    out_ref[2] = v_ref[...]


def grads_body(core, mine_ref, other_ref, out_ref):
    out_ref[core[0]] = mine_ref[...]
    out_ref[1 - core[0]] = other_ref[...]


def local_body(core, q_ref, k_ref, v_ref, other_ref, both_ref, sum_ref, first_ref):
    me = core[0]
    both_ref[0, me] = q_ref[...]
    both_ref[1, me] = k_ref[...]
    both_ref[2, me] = v_ref[...]
    for part in range(3):
        both_ref[part, 1 - me] = other_ref[part]
    total, total_norm = None, None
    for block in range(2):
        k_feat = features_of(both_ref[1, block])
        state = dot(k_feat, both_ref[2, block], TN)
        norm = jnp.sum(k_feat.astype(F32), axis=0, keepdims=True)
        if block == 0:
            put_state(first_ref, state, norm)
            total, total_norm = state, norm
        else:
            put_state(sum_ref, total + state, total_norm + norm)


def scan_body(backward, core, in_ref, out_ref):
    count = in_ref.shape[0]
    so_far = jnp.zeros(in_ref.shape[1:], F32)
    order = range(count - 1, -1, -1) if backward else range(count)
    for position in order:
        out_ref[position] = so_far
        so_far = so_far + in_ref[position]


def forward_body(core, both_ref, in_ref, first_ref, att_ref, o_ref, den_ref):
    causal = causal_mask()
    state, norm = state_of(in_ref)
    for block in range(2):
        if block == 1:
            extra, extra_norm = state_of(first_ref)
            state, norm = state + extra, norm + extra_norm
        q_feat = features_of(both_ref[0, block])
        k_feat = features_of(both_ref[1, block])
        scores = jnp.where(causal, dot(q_feat, k_feat, NT), 0.0)
        den = jnp.sum(scores, axis=1, keepdims=True) + jnp.sum(
            q_feat.astype(F32) * norm, axis=1, keepdims=True
        )
        high, low = split(state)
        out = (
            dot(scores.astype(BF), both_ref[2, block], NN)
            + dot(q_feat, high, NN)
            + dot(q_feat, low, NN)
        ) / den
        att_ref[0, block * BLK : (block + 1) * BLK] = out.astype(BF)
        o_ref[block] = out
        den_ref[block] = jnp.broadcast_to(den, (BLK, DH))


def scaled_body(
    core, w_ref, og_ref, ogr_ref, q_ref, o_ref, den_ref, g_ref, r_ref, sum_ref, last_ref
):
    me = core[0]
    g_ref[me] = dot(og_ref[...], w_ref[...], NT)
    g_ref[1 - me] = dot(ogr_ref[...], w_ref[...], NT)
    total, total_norm = None, None
    for block in range(2):
        scaled = g_ref[block] / den_ref[block]
        g_ref[block] = scaled
        residue = -jnp.sum(scaled * o_ref[block], axis=1, keepdims=True)
        r_ref[block] = jnp.broadcast_to(residue, (BLK, DH))
        q_feat = features_of(q_ref[0, block])
        high, low = split(scaled)
        state = dot(q_feat, high, TN) + dot(q_feat, low, TN)
        norm = jnp.sum(residue * q_feat.astype(F32), axis=0, keepdims=True)
        if block == 0:
            total, total_norm = state, norm
        else:
            put_state(last_ref, state, norm)
            put_state(sum_ref, total + state, total_norm + norm)


def backward_body(
    core,
    both_ref,
    in_ref,
    first_ref,
    g_ref,
    r_ref,
    later_ref,
    last_ref,
    keep_ref,
    send_ref,
    held,
):
    me = core[0]
    causal = causal_mask()
    state0, norm0 = state_of(in_ref)
    extra, extra_norm = state_of(first_ref)
    grad1, weight1 = state_of(later_ref)
    after, after_norm = state_of(last_ref)
    states = (state0, state0 + extra)
    norms = (norm0, norm0 + extra_norm)
    grads = (grad1 + after, grad1)
    weights = (weight1 + after_norm, weight1)
    for block in range(2):
        q_raw = both_ref[0, block].astype(F32)
        k_raw = both_ref[1, block].astype(F32)
        v_full = both_ref[2, block]
        q_feat, k_feat = feature(q_raw).astype(BF), feature(k_raw).astype(BF)
        scaled, residue = g_ref[block], r_ref[block]
        g_high, g_low = split(scaled)
        s_high, s_low = split(states[block])
        grad_high, grad_low = split(grads[block])
        scores = jnp.where(causal, dot(q_feat, k_feat, NT), 0.0).astype(BF)
        mixed = jnp.where(causal, dot(g_high, v_full, NT) + residue, 0.0).astype(BF)
        q_grad = (
            dot(mixed, k_feat, NN)
            + (dot(g_high, s_high, NT) + dot(g_high, s_low, NT) + dot(g_low, s_high, NT))
            + residue * norms[block]
        )
        k_grad = (
            dot(mixed, q_feat, TN)
            + (dot(v_full, grad_high, NT) + dot(v_full, grad_low, NT))
            + weights[block]
        )
        v_grad = dot(scores, g_high, TN) + (
            dot(k_feat, grad_high, NN) + dot(k_feat, grad_low, NN)
        )
        held[block, 0] = (q_grad * feature_slope(q_raw)).astype(BF)
        held[block, 1] = (k_grad * feature_slope(k_raw)).astype(BF)
        held[block, 2] = v_grad.astype(BF)
    keep_ref[...] = held[me]
    send_ref[...] = held[1 - me]


def merge_body(core, keep_ref, back_ref, q_ref, k_ref, v_ref):
    mine = pl.ds(pl.multiple_of(core[0] * DH, DH), DH)
    other = pl.ds(pl.multiple_of((1 - core[0]) * DH, DH), DH)
    for part, ref in enumerate((q_ref, k_ref, v_ref)):
        ref[:, mine] = keep_ref[part]
        ref[:, other] = back_ref[part]


def weight_body(core, mine_ref, other_ref, og_ref, out_ref):
    mine = pl.ds(pl.multiple_of(core[0] * DH, DH), DH)
    other = pl.ds(pl.multiple_of((1 - core[0]) * DH, DH), DH)
    out_ref[mine, :] = dot(mine_ref[...], og_ref[...], TN)
    out_ref[other, :] = dot(other_ref[...], og_ref[...], TN)


def total_body(core, in_ref, keep_ref, send_ref, held):
    held[...] = jnp.sum(in_ref[...], axis=0)
    keep_ref[...] = held[pl.ds(pl.multiple_of(core[0] * 8, 8), 8), :]
    send_ref[...] = held[pl.ds(pl.multiple_of((1 - core[0]) * 8, 8), 8), :]


def on_device(nx, ny, nz, queries, keys, values, out_grad, out_weight):
    chips = nx * ny
    tok, width = queries.shape[1:]
    pairs = width // (2 * DH)
    wide = width // 2
    model = out_grad.shape[2]
    half = model // 2
    me = lax.axis_index("c")
    core = jnp.reshape(me, (1,)).astype(jnp.int32)
    q_in, k_in, v_in, og = (
        part.reshape(tok, part.shape[2]) for part in (queries, keys, values, out_grad)
    )
    swap = functools.partial(lax.ppermute, axis_name="c", perm=[(0, 1), (1, 0)])
    plane = ("x", "y")

    sent = call(
        pack_body,
        (pairs,),
        [((tok, DH), lambda j, c: (0, 2 * j + 1 - c[0]))] * 3,
        [((3, tok, DH), lambda j, c: (0, 0, j), (3, tok, wide), BF)],
    )(core, q_in, k_in, v_in)[0]
    other_in = swap(sent)
    og_other = swap(og)

    moves = []
    for x in range(nx):
        for y in range(ny):
            for c in range(2):
                place = (x % (nx // 2)) * ny * 2 + y * 2 + c
                to = place * 2 + x // (nx // 2)
                moves.append((x * ny * 2 + y * 2 + c, to))
    rows = lax.ppermute(out_weight, ("x", "y", "c"), moves)
    weight = lax.all_gather(rows, ("z", "x", "y"), axis=0, tiled=True)

    col = lambda j, c: (0, 0, j)
    col4 = lambda j, c: (0, 0, 0, j)
    lead = lambda j, c: (j, 0, 0)
    state_spec = ((2, ROWS, DH), lead)
    state_out = (2, ROWS, DH), lead, (2 * pairs, ROWS, DH), F32
    pair_spec = ((2, tok, DH), col)
    pair_out = (2, tok, DH), col, (2, tok, wide), F32

    og_half = call(
        grads_body,
        (half // 512,),
        [((tok, 512), lambda j, c: (0, (half // 512) * c[0] + j))] * 2,
        [((2, tok, 512), col, (2, tok, half), BF)],
    )(core, og, og_other)[0]
    og_all = lax.all_gather(og_half.reshape(2 * tok, half), "z", axis=0, tiled=True)

    both, local_sum, first = call(
        local_body,
        (pairs,),
        [((tok, DH), lambda j, c: (0, 2 * j + c[0]))] * 3 + [((3, tok, DH), col)],
        [((3, 2, tok, DH), col4, (3, 2, tok, wide), BF), state_out, state_out],
    )(core, q_in, k_in, v_in, other_in)

    def carried_in(state, backward):
        parts = lax.all_to_all(state, plane, 0, 0, tiled=True)
        whole = ((chips, ROWS, DH), lambda j, c: (0, 0, 0))
        carried = call(
            functools.partial(scan_body, backward),
            (1,),
            [whole],
            [(*whole, (chips, ROWS, DH), F32)],
        )(core, parts)[0]
        return lax.all_to_all(carried, plane, 0, 0, tiled=True)

    earlier = carried_in(local_sum, False)
    attended, outputs, dens = call(
        forward_body,
        (pairs,),
        [((3, 2, tok, DH), col4), state_spec, state_spec],
        [((1, 2 * tok, DH), lead, (pairs, 2 * tok, DH), BF), pair_out, pair_out],
    )(core, both, earlier, first)

    att_mine = lax.all_to_all(attended, "z", 0, 0, tiled=True)
    att_other = swap(att_mine)
    tokens = nz * 2 * tok
    partial = call(
        weight_body,
        (half // 256,),
        [
            ((tokens, DH), lambda j, c: (0, 0)),
            ((tokens, DH), lambda j, c: (0, 0)),
            ((tokens, 256), lambda j, c: (0, j)),
        ],
        [((2 * DH, 256), lambda j, c: (0, j), (2 * DH, half), F32)],
    )(core, att_mine.reshape(tokens, DH), att_other.reshape(tokens, DH), og_all)[0]
    pieces = lax.all_to_all(
        partial.reshape(chips, 2 * DH // chips, half), plane, 0, 0, tiled=True
    )
    rows_each = 2 * DH // chips
    kept, moved = call(
        total_body,
        (1,),
        [((chips, rows_each, half), lambda j, c: (0, 0, 0))],
        [((rows_each // 2, half), lambda j, c: (0, 0), (rows_each // 2, half), F32)] * 2,
        [pltpu.VMEM((rows_each, half), F32)],
    )(core, pieces)
    got = swap(moved)
    weight_grad = jnp.where(
        me == 0, jnp.concatenate([kept, got], axis=1), jnp.concatenate([got, kept], axis=1)
    )

    scaled, residue, grad_sum, last = call(
        scaled_body,
        (pairs,),
        [
            ((DH, model), lambda j, c: (j, 0)),
            ((tok, model), lambda j, c: (0, 0)),
            ((tok, model), lambda j, c: (0, 0)),
            ((1, 2, tok, DH), col4),
            pair_spec,
            pair_spec,
        ],
        [pair_out, pair_out, state_out, state_out],
    )(core, weight, og, og_other, both, outputs, dens)
    later = carried_in(grad_sum, True)
    keep, send = call(
        backward_body,
        (pairs,),
        [
            ((3, 2, tok, DH), col4),
            state_spec,
            state_spec,
            pair_spec,
            pair_spec,
            state_spec,
            state_spec,
        ],
        [((3, tok, DH), col, (3, tok, wide), BF)] * 2,
        [pltpu.VMEM((2, 3, tok, DH), BF)],
    )(core, both, earlier, first, scaled, residue, later, last)
    back = swap(send)
    grads = call(
        merge_body,
        (pairs,),
        [((3, tok, DH), col)] * 2,
        [((tok, 2 * DH), lambda j, c: (0, j), (tok, width), BF)] * 3,
    )(core, keep, back)
    return (*(grad.reshape(1, tok, width) for grad in grads), weight_grad)


def solution(mesh):
    nz, nx, ny = mesh.shape["dp"], 4, mesh.shape["seq"] // 8
    grid = Mesh(mesh.devices.reshape(nz, nx, ny, 2), ("z", "x", "y", "c"))
    tokens = P("z", ("x", "y", "c"), None)
    weights = P(("z", "x", "y", "c"), None)
    return jax.shard_map(
        functools.partial(on_device, nx, ny, nz),
        mesh=grid,
        in_specs=(tokens, tokens, tokens, tokens, weights),
        out_specs=(tokens, tokens, tokens, weights),
        check_vma=False,
    )
```

```python
import functools

import jax
import jax.numpy as jnp
from jax import lax
from jax.experimental import pallas as pl
from jax.experimental.pallas import tpu as pltpu
from jax.sharding import Mesh, PartitionSpec as P

DH = 128
BLK = 128
BF = jnp.bfloat16
F32 = jnp.float32
NN = (((1,), (0,)), ((), ()))
NT = (((1,), (1,)), ((), ()))
TN = (((0,), (0,)), ((), ()))
HALF = DH // 2
ROWS = HALF + 8
PARAMS = pltpu.CompilerParams(vmem_limit_bytes=16 * 1024 * 1024)


def dot(left, right, dims):
    return lax.dot_general(left, right, dims, preferred_element_type=F32)


def split(wide):
    high = wide.astype(BF)
    return high, (wide - high.astype(F32)).astype(BF)


def feature(raw):
    return jnp.where(raw > 0, raw + 1.0, jnp.exp(jnp.minimum(raw, 0.0)))


def feature_slope(raw):
    return jnp.where(raw > 0, 1.0, jnp.exp(jnp.minimum(raw, 0.0)))


def features_of(raw):
    return feature(raw.astype(F32)).astype(BF)


def causal_mask():
    row = lax.broadcasted_iota(jnp.int32, (BLK, BLK), 0)
    col = lax.broadcasted_iota(jnp.int32, (BLK, BLK), 1)
    return row >= col


def state_of(ref):
    return jnp.concatenate([ref[0, :HALF], ref[1, :HALF]], axis=0), ref[0, HALF : HALF + 1]


def put_state(ref, matrix, vector):
    tail = jnp.broadcast_to(vector, (8, DH))
    for half in range(2):
        ref[half, :HALF] = matrix[half * HALF : (half + 1) * HALF]
        ref[half, HALF:] = tail


def call(body, grid, ins, outs, scratch=()):
    run = pl.pallas_call(
        body,
        grid_spec=pltpu.PrefetchScalarGridSpec(
            num_scalar_prefetch=1,
            grid=grid,
            in_specs=[pl.BlockSpec(*spec) for spec in ins],
            out_specs=[pl.BlockSpec(spec[0], spec[1]) for spec in outs],
            scratch_shapes=list(scratch),
        ),
        out_shape=[pltpu.HBM(spec[2], spec[3]) for spec in outs],
        compiler_params=PARAMS,
    )

    return run


def kept_out(*arrays):
    return [pltpu.with_memory_space_constraint(array, pltpu.HBM) for array in arrays]


def put_pair(ref, core, mine, other):
    ref[core] = mine[...]
    ref[1 - core] = other[...]


def local_body(place, k_ref, v_ref, k_other, v_other, keys, values, sum_ref, first_ref):
    put_pair(keys, place[0], k_ref, k_other)
    put_pair(values, place[0], v_ref, v_other)
    total, total_norm = None, None
    for block in range(2):
        k_feat = features_of(keys[block])
        state = dot(k_feat, values[block], TN)
        norm = jnp.sum(k_feat.astype(F32), axis=0, keepdims=True)
        if block == 0:
            put_state(first_ref, state, norm)
            total, total_norm = state, norm
        else:
            put_state(sum_ref, total + state, total_norm + norm)


def scan_body(backward, place, in_ref, out_ref):
    count = in_ref.shape[0]
    so_far = jnp.zeros(in_ref.shape[1:], F32)
    order = range(count - 1, -1, -1) if backward else range(count)
    for position in order:
        out_ref[position] = so_far
        so_far = so_far + in_ref[position]


def attn_grad_body(place, og_ref, w_ref, out_ref):
    out_ref[0] = dot(og_ref[...], w_ref[...], NT).astype(BF)


def forward_body(
    place,
    q_ref,
    q_other,
    keys,
    values,
    in_ref,
    first_ref,
    queries,
    copy_ref,
    att_ref,
    o_ref,
    den_ref,
):
    put_pair(queries, place[0], q_ref, q_other)
    copy_ref[...] = in_ref[...]
    causal = causal_mask()
    state, norm = state_of(in_ref)
    for block in range(2):
        if block == 1:
            extra, extra_norm = state_of(first_ref)
            state, norm = state + extra, norm + extra_norm
        q_feat = features_of(queries[block])
        k_feat = features_of(keys[block])
        scores = jnp.where(causal, dot(q_feat, k_feat, NT), 0.0)
        den = jnp.sum(scores, axis=1, keepdims=True) + jnp.sum(
            q_feat.astype(F32) * norm, axis=1, keepdims=True
        )
        high, low = split(state)
        out = (
            dot(scores.astype(BF), values[block], NN)
            + dot(q_feat, high, NN)
            + dot(q_feat, low, NN)
        ) / den
        att_ref[0, block * BLK : (block + 1) * BLK] = out.astype(BF)
        o_ref[block] = out
        den_ref[block] = jnp.broadcast_to(den, (BLK, DH))


def scaled_body(
    place,
    queries,
    o_ref,
    den_ref,
    grad_ref,
    grad_other,
    g_ref,
    r_ref,
    sum_ref,
    last_ref,
    grads,
):
    me = place[0]
    grads[me] = grad_ref[0]
    grads[1 - me] = grad_other[0]
    total, total_norm = None, None
    for block in range(2):
        q_feat = features_of(queries[block])
        scaled = grads[block].astype(F32) / den_ref[block]
        g_ref[block] = scaled
        residue = -jnp.sum(scaled * o_ref[block], axis=1, keepdims=True)
        r_ref[block] = jnp.broadcast_to(residue, (BLK, DH))
        high, low = split(scaled)
        grad = dot(q_feat, high, TN) + dot(q_feat, low, TN)
        grad_norm = jnp.sum(residue * q_feat.astype(F32), axis=0, keepdims=True)
        if block == 0:
            total, total_norm = grad, grad_norm
        else:
            put_state(last_ref, grad, grad_norm)
            put_state(sum_ref, total + grad, total_norm + grad_norm)


def backward_body(
    place,
    queries,
    keys,
    values,
    in_ref,
    first_ref,
    g_ref,
    r_ref,
    later_ref,
    last_ref,
    keep_ref,
    send_ref,
    held,
):
    me = place[0]
    causal = causal_mask()
    state0, norm0 = state_of(in_ref)
    extra, extra_norm = state_of(first_ref)
    grad1, weight1 = state_of(later_ref)
    after, after_norm = state_of(last_ref)
    states = (state0, state0 + extra)
    norms = (norm0, norm0 + extra_norm)
    grads = (grad1 + after, grad1)
    weights = (weight1 + after_norm, weight1)
    for block in range(2):
        q_raw = queries[block].astype(F32)
        k_raw = keys[block].astype(F32)
        v_full = values[block]
        q_feat, k_feat = feature(q_raw).astype(BF), feature(k_raw).astype(BF)
        scaled, residue = g_ref[block], r_ref[block]
        g_high, g_low = split(scaled)
        s_high, s_low = split(states[block])
        grad_high, grad_low = split(grads[block])
        scores = jnp.where(causal, dot(q_feat, k_feat, NT), 0.0).astype(BF)
        mixed = jnp.where(causal, dot(g_high, v_full, NT) + residue, 0.0).astype(BF)
        q_grad = (
            dot(mixed, k_feat, NN)
            + (dot(g_high, s_high, NT) + dot(g_high, s_low, NT) + dot(g_low, s_high, NT))
            + residue * norms[block]
        )
        k_grad = (
            dot(mixed, q_feat, TN)
            + (dot(v_full, grad_high, NT) + dot(v_full, grad_low, NT))
            + weights[block]
        )
        v_grad = dot(scores, g_high, TN) + (
            dot(k_feat, grad_high, NN) + dot(k_feat, grad_low, NN)
        )
        held[block, 0] = (q_grad * feature_slope(q_raw)).astype(BF)
        held[block, 1] = (k_grad * feature_slope(k_raw)).astype(BF)
        held[block, 2] = v_grad.astype(BF)
    keep_ref[...] = held[me]
    send_ref[...] = held[1 - me]


def merge_body(place, keep_ref, back_ref, q_ref, k_ref, v_ref):
    mine = pl.ds(pl.multiple_of(place[0] * DH, DH), DH)
    other = pl.ds(pl.multiple_of((1 - place[0]) * DH, DH), DH)
    for part, ref in enumerate((q_ref, k_ref, v_ref)):
        ref[:, mine] = keep_ref[part]
        ref[:, other] = back_ref[part]


def weight_body(steps, place, mine_ref, other_ref, og_ref, send_ref, keep_ref, heads):
    left = pl.ds(pl.multiple_of(place[0] * DH, DH), DH)
    right = pl.ds(pl.multiple_of((1 - place[0]) * DH, DH), DH)

    @pl.when(pl.program_id(0) == 0)
    def _():
        heads[:, left] = mine_ref[...].reshape(-1, DH)
        heads[:, right] = other_ref[...].reshape(-1, DH)

    part = dot(heads[...], og_ref[...], TN)

    @pl.when(pl.program_id(0) < steps)
    def _():
        send_ref[...] = part

    @pl.when(pl.program_id(0) >= steps)
    def _():
        keep_ref[...] = part


def total_body(place, in_ref, keep_ref, send_ref, held):
    held[...] = jnp.sum(in_ref[...], axis=0)
    keep_ref[...] = held[pl.ds(pl.multiple_of(place[0] * 8, 8), 8), :]
    send_ref[...] = held[pl.ds(pl.multiple_of((1 - place[0]) * 8, 8), 8), :]


def on_device(nx, ny, nz, queries, keys, values, out_grad, out_weight):
    chips = nx * ny
    tok, width = queries.shape[1:]
    pairs = width // (2 * DH)
    wide = width // 2
    model = out_grad.shape[2]
    half = model // 2
    me = lax.axis_index("c")
    place = jnp.stack([lax.axis_index(name) for name in ("c", "x", "y", "z")]).astype(jnp.int32)
    q_in, k_in, v_in, og = (
        part.reshape(tok, part.shape[2]) for part in (queries, keys, values, out_grad)
    )
    swap = functools.partial(lax.ppermute, axis_name="c", perm=[(0, 1), (1, 0)])
    plane = ("x", "y")

    k_other, v_other, q_other = swap(k_in), swap(v_in), swap(q_in)
    og_all = lax.all_gather(og, "z", axis=0, tiled=True)

    col = lambda j, p: (0, 0, j)
    lead = lambda j, p: (j, 0, 0)
    state_spec = ((2, ROWS, DH), lead)
    state_out = (2, ROWS, DH), lead, (2 * pairs, ROWS, DH), F32
    pair_spec = ((2, tok, DH), col)
    pair_out = (2, tok, DH), col, (2, tok, wide), F32
    head_spec = ((tok, DH), lambda j, p: (0, 2 * j + p[0]))
    pair_hold = pltpu.VMEM((2, tok, DH), BF)

    both_out = (2, tok, DH), col, (2, tok, wide), BF
    keys_all, values_all, local_sum, first = call(
        local_body,
        (pairs,),
        [head_spec] * 4,
        [both_out, both_out, state_out, state_out],
    )(place, *kept_out(k_in, v_in), k_other, v_other)
    keys_all, values_all, first = kept_out(keys_all, values_all, first)

    spread = jnp.broadcast_to(out_weight[None], (chips, *out_weight.shape))
    rows_mine = lax.all_to_all(spread, plane, 0, 0, tiled=True)
    rows_mine, local_sum = lax.optimization_barrier((rows_mine, local_sum))

    def carried_in(state, backward):
        parts = lax.all_to_all(state, plane, 0, 0, tiled=True)
        whole = ((chips, ROWS, DH), lambda j, p: (0, 0, 0))
        carried = call(
            functools.partial(scan_body, backward),
            (1,),
            [whole],
            [(*whole, (chips, ROWS, DH), F32)],
        )(place, parts)[0]
        return lax.all_to_all(carried, plane, 0, 0, tiled=True)

    earlier = carried_in(local_sum, False)
    queries_all, earlier, attended, outputs, dens = call(
        forward_body,
        (pairs,),
        [head_spec] * 2 + [pair_spec] * 2 + [state_spec] * 2,
        [both_out, state_out]
        + [((1, 2 * tok, DH), lead, (pairs, 2 * tok, DH), BF), pair_out, pair_out],
    )(place, *kept_out(q_in), q_other, keys_all, values_all, earlier, first)

    og_all = lax.optimization_barrier((og_all, attended))[0]
    og_all = kept_out(og_all)[0]
    rows_other = swap(rows_mine)
    rows = jnp.where(
        me == 0,
        jnp.stack([rows_mine, rows_other], axis=1),
        jnp.stack([rows_other, rows_mine], axis=1),
    ).reshape(2 * DH, model)
    attn_grad = call(
        attn_grad_body,
        (nz,),
        [((tok, model), lambda k, p: (k, 0)), ((2 * DH, model), lambda k, p: (0, 0))],
        [((1, tok, 2 * DH), lead, (nz, tok, 2 * DH), BF)],
    )(place, og_all, rows)[0]
    att_mine = lax.all_to_all(attended, "z", 0, 0, tiled=True)
    attn_grad, att_mine = lax.optimization_barrier((attn_grad, att_mine))
    grad_mine = lax.all_to_all(attn_grad, "z", 0, 0, tiled=True)
    grad_other = swap(grad_mine)
    grad_spec = ((1, tok, DH), lambda j, p: (j, 0, p[0]))
    scaled, residue, grad_sum, last = call(
        scaled_body,
        (pairs,),
        [pair_spec] * 3 + [grad_spec] * 2,
        [pair_out, pair_out, state_out, state_out],
        [pair_hold],
    )(place, *kept_out(queries_all, outputs, dens), grad_mine, grad_other)

    att_other = swap(att_mine)
    steps = half // 256
    att_spec = ((nz, tok, DH), lambda j, p: (0, p[0], 0))
    moved, kept = call(
        functools.partial(weight_body, steps),
        (2 * steps,),
        [
            att_spec,
            att_spec,
            (
                (nz * tok, 256),
                lambda j, p: (0, jnp.where(j < steps, 1 - p[0], p[0]) * steps + lax.rem(j, steps)),
            ),
        ],
        [
            ((2 * DH, 256), lambda j, p: (0, jnp.minimum(j, steps - 1)), (2 * DH, half), F32),
            ((2 * DH, 256), lambda j, p: (0, jnp.maximum(j - steps, 0)), (2 * DH, half), F32),
        ],
        [pltpu.VMEM((nz * tok, 2 * DH), BF)],
    )(place, att_mine, att_other, og_all)
    partial = kept + swap(moved)
    rows_each = 2 * DH // chips
    pieces = lax.all_to_all(
        partial.reshape(chips, rows_each, half), plane, 0, 0, tiled=True
    )
    kept, moved = call(
        total_body,
        (1,),
        [((chips, rows_each, half), lambda j, p: (0, 0, 0))],
        [((rows_each // 2, half), lambda j, p: (0, 0), (rows_each // 2, half), F32)] * 2,
        [pltpu.VMEM((rows_each, half), F32)],
    )(place, pieces)
    got = swap(moved)
    weight_grad = jnp.where(
        me == 0, jnp.concatenate([kept, got], axis=1), jnp.concatenate([got, kept], axis=1)
    )

    later = carried_in(grad_sum, True)
    keep, send = call(
        backward_body,
        (pairs,),
        [pair_spec] * 3
        + [state_spec, state_spec, pair_spec, pair_spec, state_spec, state_spec],
        [((3, tok, DH), col, (3, tok, wide), BF)] * 2,
        [pltpu.VMEM((2, 3, tok, DH), BF)],
    )(
        place,
        *kept_out(queries_all, keys_all, values_all, earlier, first, scaled, residue),
        later,
        *kept_out(last),
    )
    back = swap(send)
    grads = call(
        merge_body,
        (pairs,),
        [((3, tok, DH), col)] * 2,
        [((tok, 2 * DH), lambda j, p: (0, j), (tok, width), BF)] * 3,
    )(place, *kept_out(keep), back)
    return (*(grad.reshape(1, tok, width) for grad in grads), weight_grad)


def solution(mesh):
    nz, nx, ny = mesh.shape["dp"], 4, mesh.shape["seq"] // 8
    grid = Mesh(mesh.devices.reshape(nz, nx, ny, 2), ("z", "x", "y", "c"))
    tokens = P("z", ("x", "y", "c"), None)
    weights = P(("z", "x", "y", "c"), None)
    return jax.shard_map(
        functools.partial(on_device, nx, ny, nz),
        mesh=grid,
        in_specs=(tokens, tokens, tokens, tokens, weights),
        out_specs=(tokens, tokens, tokens, weights),
        check_vma=False,
    )
```

```python
import functools

import jax
import jax.numpy as jnp
from jax import lax
from jax.experimental import pallas as pl
from jax.experimental.pallas import tpu as pltpu
from jax.sharding import Mesh, PartitionSpec as P

DH = 128
BLK = 128
BF = jnp.bfloat16
F32 = jnp.float32
NN = (((1,), (0,)), ((), ()))
NT = (((1,), (1,)), ((), ()))
TN = (((0,), (0,)), ((), ()))
HALF = DH // 2
ROWS = HALF + 8
PARAMS = pltpu.CompilerParams(vmem_limit_bytes=24 * 1024 * 1024)


def dot(left, right, dims):
    return lax.dot_general(left, right, dims, preferred_element_type=F32)


def split(wide):
    high = wide.astype(BF)
    return high, (wide - high.astype(F32)).astype(BF)


def feature(raw):
    return jnp.where(raw > 0, raw + 1.0, jnp.exp(jnp.minimum(raw, 0.0)))


def feature_slope(raw):
    return jnp.where(raw > 0, 1.0, jnp.exp(jnp.minimum(raw, 0.0)))


def features_of(raw):
    return feature(raw.astype(F32)).astype(BF)


def causal_mask():
    row = lax.broadcasted_iota(jnp.int32, (BLK, BLK), 0)
    col = lax.broadcasted_iota(jnp.int32, (BLK, BLK), 1)
    return row >= col


def state_of(ref, head):
    low, high = 2 * head, 2 * head + 1
    matrix = jnp.concatenate([ref[low, :HALF], ref[high, :HALF]], axis=0)
    return matrix, ref[low, HALF : HALF + 1]


def put_state(ref, head, matrix, vector):
    tail = jnp.broadcast_to(vector, (8, DH))
    for half in range(2):
        ref[2 * head + half, :HALF] = matrix[half * HALF : (half + 1) * HALF]
        ref[2 * head + half, HALF:ROWS] = tail


def call(body, grid, ins, outs, scratch=()):
    run = pl.pallas_call(
        body,
        grid_spec=pltpu.PrefetchScalarGridSpec(
            num_scalar_prefetch=1,
            grid=grid,
            in_specs=[pl.BlockSpec(*spec[:2], memory_space=(spec[2:] or (None,))[0]) for spec in ins],
            out_specs=[pl.BlockSpec(spec[0], spec[1]) for spec in outs],
            scratch_shapes=list(scratch),
        ),
        out_shape=[pltpu.HBM(spec[2], spec[3]) for spec in outs],
        compiler_params=PARAMS,
    )

    return run


def kept_out(*arrays):
    return [pltpu.with_memory_space_constraint(array, pltpu.HBM) for array in arrays]


def put_pair(ref, head, core, mine, other):
    cols = pl.ds(pl.multiple_of((2 * head + core) * DH, DH), DH)
    ref[head, core] = mine[:, cols]
    ref[head, 1 - core] = other[:, cols]


def local_body(place, k_ref, v_ref, k_other, v_other, keys, values, sum_ref, first_ref):
    for head in range(keys.shape[0]):
        put_pair(keys, head, place[0], k_ref, k_other)
        put_pair(values, head, place[0], v_ref, v_other)
    for head in range(keys.shape[0]):
        feats = [features_of(keys[head, block]) for block in range(2)]
        states = [dot(feats[block], values[head, block], TN) for block in range(2)]
        norms = [jnp.sum(feat.astype(F32), axis=0, keepdims=True) for feat in feats]
        put_state(first_ref, head, states[0], norms[0])
        put_state(sum_ref, head, states[0] + states[1], norms[0] + norms[1])


def scan_body(place, in_ref, out_ref):
    count = in_ref.shape[0]
    so_far = jnp.zeros(in_ref.shape[1:], F32)
    for position in range(count):
        out_ref[position] = so_far
        so_far = so_far + in_ref[position]


def back_scan_body(place, in_ref, out_ref):
    count = in_ref.shape[0]
    so_far = jnp.zeros(in_ref.shape[1:], F32)
    for position in range(count - 1, -1, -1):
        out_ref[position] = so_far
        so_far = so_far + in_ref[position]


def total_body(place, in_ref, keep_ref, send_ref):
    total = in_ref[0].astype(F32)
    for position in range(1, in_ref.shape[0]):
        total = total + in_ref[position].astype(F32)
    low, high = total[:8], total[8:]
    keep_ref[...] = jnp.where(place[0] == 0, low, high)
    send_ref[...] = jnp.where(place[0] == 0, high, low)


def attn_grad_body(count, place, *refs):
    *og_refs, w_ref, out_ref, tokens, arrived = refs
    copies, start = [], 0
    for position, ref in enumerate(og_refs):
        here = tokens.at[pl.ds(start, ref.shape[0])]
        copies.append(pltpu.make_async_copy(ref, here, arrived.at[position]))
        copies[-1].start()
        start += ref.shape[0]
    batch = count // 2
    for first, waits in ((0, copies[:batch]), (batch, copies[batch:])):
        for copy in waits:
            copy.wait()
        part = dot(tokens[first * BLK : (first + batch) * BLK], w_ref[...], NT).astype(BF)
        for more in range(batch):
            out_ref[lax.rem(place[3] + first + more, count)] = part[more * BLK : (more + 1) * BLK]


def forward_body(
    place,
    q_ref,
    q_other,
    keys,
    values,
    in_ref,
    first_ref,
    queries,
    copy_ref,
    att_ref,
    o_ref,
    den_ref,
):
    copy_ref[...] = in_ref[...]
    causal = causal_mask()
    for head in range(keys.shape[0]):
        put_pair(queries, head, place[0], q_ref, q_other)
    for head in range(keys.shape[0]):
        state, norm = state_of(in_ref, head)
        extra, extra_norm = state_of(first_ref, head)
        for block in range(2):
            if block == 1:
                state, norm = state + extra, norm + extra_norm
            q_feat = features_of(queries[head, block])
            k_feat = features_of(keys[head, block])
            scores = jnp.where(causal, dot(q_feat, k_feat, NT), 0.0)
            den = jnp.sum(scores, axis=1, keepdims=True) + jnp.sum(
                q_feat.astype(F32) * norm, axis=1, keepdims=True
            )
            high, low = split(state)
            out = (
                dot(scores.astype(BF), values[head, block], NN)
                + dot(q_feat, high, NN)
                + dot(q_feat, low, NN)
            ) / den
            att_ref[head, block * BLK : (block + 1) * BLK] = out.astype(BF)
            o_ref[head, block] = out
            den_ref[head, block] = jnp.broadcast_to(den, (BLK, DH))


def scaled_body(
    place,
    queries,
    o_ref,
    den_ref,
    grad_ref,
    grad_other,
    g_ref,
    r_ref,
    sum_ref,
    last_ref,
    grads,
):
    me = place[0]
    cols = pl.ds(pl.multiple_of(me * DH, DH), DH)
    for head in range(queries.shape[0]):
        grads[head, me] = grad_ref[head, :, cols]
        grads[head, 1 - me] = grad_other[head, :, cols]
    for head in range(queries.shape[0]):
        sums, norms = [], []
        for block in range(2):
            q_feat = features_of(queries[head, block])
            scaled = grads[head, block].astype(F32) / den_ref[head, block]
            g_ref[head, block] = scaled
            residue = -jnp.sum(scaled * o_ref[head, block], axis=1, keepdims=True)
            r_ref[head, block] = jnp.broadcast_to(residue, (BLK, DH))
            high, low = split(scaled)
            sums.append(dot(q_feat, high, TN) + dot(q_feat, low, TN))
            norms.append(jnp.sum(residue * q_feat.astype(F32), axis=0, keepdims=True))
        put_state(last_ref, head, sums[1], norms[1])
        put_state(sum_ref, head, sums[0] + sums[1], norms[0] + norms[1])


def backward_body(
    place,
    queries,
    keys,
    values,
    in_ref,
    first_ref,
    g_ref,
    r_ref,
    later_ref,
    last_ref,
    keep_ref,
    send_ref,
    held,
):
    me = place[0]
    causal = causal_mask()
    for head in range(keys.shape[0]):
        state0, norm0 = state_of(in_ref, head)
        extra, extra_norm = state_of(first_ref, head)
        grad1, weight1 = state_of(later_ref, head)
        after, after_norm = state_of(last_ref, head)
        states = (state0, state0 + extra)
        norms = (norm0, norm0 + extra_norm)
        grads = (grad1 + after, grad1)
        weights = (weight1 + after_norm, weight1)
        for block in range(2):
            q_raw = queries[head, block].astype(F32)
            k_raw = keys[head, block].astype(F32)
            v_full = values[head, block]
            q_feat, k_feat = feature(q_raw).astype(BF), feature(k_raw).astype(BF)
            scaled, residue = g_ref[head, block], r_ref[head, block]
            g_high, g_low = split(scaled)
            s_high, s_low = split(states[block])
            grad_high, grad_low = split(grads[block])
            scores = jnp.where(causal, dot(q_feat, k_feat, NT), 0.0).astype(BF)
            mixed = jnp.where(causal, dot(g_high, v_full, NT) + residue, 0.0).astype(BF)
            q_grad = (
                dot(mixed, k_feat, NN)
                + (dot(g_high, s_high, NT) + dot(g_high, s_low, NT) + dot(g_low, s_high, NT))
                + residue * norms[block]
            )
            k_grad = (
                dot(mixed, q_feat, TN)
                + (dot(v_full, grad_high, NT) + dot(v_full, grad_low, NT))
                + weights[block]
            )
            v_grad = dot(scores, g_high, TN) + (
                dot(k_feat, grad_high, NN) + dot(k_feat, grad_low, NN)
            )
            held[block, head, 0] = (q_grad * feature_slope(q_raw)).astype(BF)
            held[block, head, 1] = (k_grad * feature_slope(k_raw)).astype(BF)
            held[block, head, 2] = v_grad.astype(BF)
    keep_ref[...] = held[me]
    send_ref[...] = held[1 - me]


def merge_body(place, keep_ref, back_ref, q_ref, k_ref, v_ref):
    for head in range(keep_ref.shape[0]):
        mine = pl.ds(pl.multiple_of((2 * head + place[0]) * DH, DH), DH)
        other = pl.ds(pl.multiple_of((2 * head + 1 - place[0]) * DH, DH), DH)
        for part, ref in enumerate((q_ref, k_ref, v_ref)):
            ref[:, mine] = keep_ref[head, part]
            ref[:, other] = back_ref[head, part]


def weight_body(steps, count, place, mine_ref, other_ref, *refs):
    *og_refs, send_ref, keep_ref, heads = refs
    left = pl.ds(pl.multiple_of(place[0] * DH, DH), DH)
    right = pl.ds(pl.multiple_of((1 - place[0]) * DH, DH), DH)

    @pl.when(pl.program_id(0) == 0)
    def _():
        for ahead in range(count):
            source = lax.rem(place[3] + ahead, count)
            heads[ahead * BLK : (ahead + 1) * BLK, left] = mine_ref[source]
            heads[ahead * BLK : (ahead + 1) * BLK, right] = other_ref[source]

    right_side = jnp.concatenate([ref[...] for ref in og_refs], axis=0)
    part = dot(heads[...], right_side, TN)

    @pl.when(pl.program_id(0) < steps)
    def _():
        send_ref[...] = part

    @pl.when(pl.program_id(0) >= steps)
    def _():
        keep_ref[...] = part


def on_device(nx, ny, nz, queries, keys, values, out_grad, out_weight):
    chips = nx * ny
    tok, width = queries.shape[1:]
    pairs = width // (2 * DH)
    model = out_grad.shape[2]
    half = model // 2
    me = lax.axis_index("c")
    place = jnp.stack([lax.axis_index(name) for name in ("c", "x", "y", "z")]).astype(jnp.int32)
    q_in, k_in, v_in, og = (
        part.reshape(tok, part.shape[2]) for part in (queries, keys, values, out_grad)
    )
    swap = functools.partial(lax.ppermute, axis_name="c", perm=[(0, 1), (1, 0)])
    plane = ("x", "y")

    def from_ahead(piece, axis, size, ahead):
        return lax.ppermute(piece, axis, [((i + ahead) % size, i) for i in range(size)])

    k_other, v_other, q_other = swap(k_in), swap(v_in), swap(q_in)

    def both_ways(up, down):
        return from_ahead(up, "z", nz, 1), from_ahead(down, "z", nz, -1)

    og_1, og_7 = both_ways(og, og)
    og_2, og_6 = both_ways(og_1, og_7)
    og_3, og_5 = both_ways(og_2, og_6)
    low, high = both_ways(og_3[: tok // 2], og_5[tok // 2 :])
    og_all = kept_out(og, og_1, og_2, og_3, low, high, og_5, og_6, og_7)

    heads = 2
    grid = (pairs // heads,)
    lead = lambda j, p: (j, 0, 0)
    lead4 = lambda j, p: (j, 0, 0, 0)
    state_spec = ((2 * heads, ROWS, DH), lead)
    state_out = (*state_spec, (2 * pairs, ROWS, DH), F32)
    pair_spec = ((heads, 2, tok, DH), lead4)
    pair_out = (*pair_spec, (pairs, 2, tok, DH), F32)
    both_out = (*pair_spec, (pairs, 2, tok, DH), BF)
    head_spec = ((tok, 2 * heads * DH), lambda j, p: (0, j))
    whole = lambda *shape: (shape, lambda j, p: (0,) * len(shape))

    keys_all, values_all, local_sum, first = call(
        local_body, grid, [head_spec] * 4, [both_out, both_out, state_out, state_out]
    )(place, *kept_out(k_in, v_in), k_other, v_other)
    keys_all, values_all, first = kept_out(keys_all, values_all, first)

    out_weight = lax.optimization_barrier((out_weight, local_sum))[0]

    def fetched(piece, axis, size):
        return [from_ahead(piece, axis, size, ahead) for ahead in range(1, size)]

    def gathered(piece, fetched_parts, start):
        size = len(fetched_parts) + 1
        whole = jnp.broadcast_to(piece[None], (size, *piece.shape))
        for ahead, part in enumerate(fetched_parts, start=1):
            place = lax.rem(start + ahead, size)
            whole = lax.dynamic_update_index_in_dim(whole, part, place, 0)
        return whole

    row_group = gathered(out_weight, fetched(out_weight, "y", ny), lax.axis_index("y"))
    row_groups = fetched(row_group, "x", nx)

    parts = lax.all_to_all(local_sum, plane, 0, 0, tiled=True)
    earlier = call(
        scan_body,
        (1,),
        [whole(chips, ROWS, DH)],
        [(*whole(chips, ROWS, DH), (chips, ROWS, DH), F32)],
    )(place, parts)[0]
    earlier = lax.all_to_all(earlier, plane, 0, 0, tiled=True)
    queries_all, earlier, attended, outputs, dens = call(
        forward_body,
        grid,
        [head_spec] * 2 + [pair_spec] * 2 + [state_spec] * 2,
        [both_out, state_out]
        + [((heads, 2 * tok, DH), lead, (pairs, 2 * tok, DH), BF), pair_out, pair_out],
    )(place, *kept_out(q_in), q_other, keys_all, values_all, earlier, first)
    row_groups = lax.optimization_barrier((row_groups, attended))[0]
    rows_mine = gathered(row_group, row_groups, lax.axis_index("x")).reshape(chips, 8, model)
    rows_other = swap(rows_mine)
    rows = jnp.where(
        me == 0,
        jnp.stack([rows_mine, rows_other], axis=1),
        jnp.stack([rows_other, rows_mine], axis=1),
    ).reshape(2 * DH, model)
    att_mine = lax.all_to_all(attended, "z", 0, 0, tiled=True)
    att_other = swap(att_mine)

    attn_grad = call(
        functools.partial(attn_grad_body, nz),
        (1,),
        [(None, None, pl.ANY)] * len(og_all) + [whole(2 * DH, model)],
        [(*whole(nz, tok, 2 * DH), (nz, tok, 2 * DH), BF)],
        [pltpu.VMEM((nz * tok, model), BF), pltpu.SemaphoreType.DMA((len(og_all),))],
    )(place, *og_all, rows)[0]
    attn_grad, att_mine = lax.optimization_barrier((attn_grad, att_mine))
    grad_mine = lax.all_to_all(attn_grad, "z", 0, 0, tiled=True)

    steps = 2
    cols = half // steps
    att_spec = ((nz, tok, DH), lambda j, p: (0, p[0], 0))
    og_col = lambda j, p: (0, jnp.where(j < steps, 1 - p[0], p[0]) * steps + lax.rem(j, steps))
    moved, kept = call(
        functools.partial(weight_body, steps, nz),
        (2 * steps,),
        [att_spec] * 2 + [((part.shape[0], cols), og_col) for part in og_all],
        [
            ((2 * DH, cols), lambda j, p: (0, jnp.minimum(j, steps - 1)), (2 * DH, half), F32),
            ((2 * DH, cols), lambda j, p: (0, jnp.maximum(j - steps, 0)), (2 * DH, half), F32),
        ],
        [pltpu.VMEM((nz * tok, 2 * DH), BF)],
    )(place, att_mine, att_other, *og_all)
    grad_mine, moved, kept = lax.optimization_barrier((grad_mine, moved, kept))
    grad_other = swap(grad_mine)
    got = swap(moved)

    grad_spec = ((heads, tok, 2 * DH), lead)
    scaled, residue, grad_sum, last = call(
        scaled_body,
        grid,
        [pair_spec] * 3 + [grad_spec] * 2,
        [pair_out, pair_out, state_out, state_out],
        [pltpu.VMEM((heads, 2, tok, DH), BF)],
    )(
        place,
        *kept_out(queries_all, outputs, dens),
        *(grad_mine, grad_other),
    )
    parts = lax.all_to_all(grad_sum, plane, 0, 0, tiled=True)
    later = call(
        back_scan_body,
        (1,),
        [whole(chips, ROWS, DH)],
        [(*whole(chips, ROWS, DH), (chips, ROWS, DH), F32)],
    )(place, parts)[0]
    later = lax.all_to_all(later, plane, 0, 0, tiled=True)
    shares = (kept + got).astype(BF).reshape(chips, 2 * DH // chips, half)
    later, shares = lax.optimization_barrier((later, shares))
    shares = lax.all_to_all(shares, plane, 0, 0, tiled=True)
    grad_out = ((heads, 3, tok, DH), lead4, (pairs, 3, tok, DH), BF)
    keep, send = call(
        backward_body,
        grid,
        [pair_spec] * 3
        + [state_spec, state_spec, pair_spec, pair_spec, state_spec, state_spec],
        [grad_out] * 2,
        [pltpu.VMEM((2, heads, 3, tok, DH), BF)],
    )(
        place,
        *kept_out(queries_all, keys_all, values_all, earlier, first, scaled, residue),
        later,
        *kept_out(last),
    )
    send, shares = lax.optimization_barrier((send, shares))
    back = swap(send)
    weight_kept, weight_moved = call(
        total_body,
        (1,),
        [whole(*shares.shape)],
        [(*whole(8, half), (8, half), F32)] * 2,
    )(place, shares)
    weight_got = swap(weight_moved)
    weight_grad = jnp.where(
        me == 0,
        jnp.concatenate([weight_kept, weight_got], axis=1),
        jnp.concatenate([weight_got, weight_kept], axis=1),
    )
    grads = call(
        merge_body,
        grid,
        [grad_out[:2]] * 2,
        [(*head_spec, (tok, width), BF)] * 3,
    )(place, *kept_out(keep), back)
    return (*(grad.reshape(1, tok, width) for grad in grads), weight_grad)


def solution(mesh):
    nz, nx, ny = mesh.shape["dp"], 4, mesh.shape["seq"] // 8
    grid = Mesh(mesh.devices.reshape(nz, nx, ny, 2), ("z", "x", "y", "c"))
    tokens = P("z", ("x", "y", "c"), None)
    weights = P(("z", "x", "y", "c"), None)
    return jax.shard_map(
        functools.partial(on_device, nx, ny, nz),
        mesh=grid,
        in_specs=(tokens, tokens, tokens, tokens, weights),
        out_specs=(tokens, tokens, tokens, weights),
        check_vma=False,
    )
```

```python
import functools

import jax
import jax.numpy as jnp
from jax import lax
from jax.experimental import pallas as pl
from jax.experimental.pallas import tpu as pltpu
from jax.sharding import Mesh, PartitionSpec as P

DH = 128
BLK = 128
BF = jnp.bfloat16
F32 = jnp.float32
NN = (((1,), (0,)), ((), ()))
NT = (((1,), (1,)), ((), ()))
TN = (((0,), (0,)), ((), ()))
HALF = DH // 2
ROWS = HALF + 8
PARAMS = pltpu.CompilerParams(vmem_limit_bytes=24 * 1024 * 1024)


def dot(left, right, dims):
    return lax.dot_general(left, right, dims, preferred_element_type=F32)


def split(wide):
    high = wide.astype(BF)
    return high, (wide - high.astype(F32)).astype(BF)


def feature(raw):
    return jnp.where(raw > 0, raw + 1.0, jnp.exp(jnp.minimum(raw, 0.0)))


def feature_slope(raw):
    return jnp.where(raw > 0, 1.0, jnp.exp(jnp.minimum(raw, 0.0)))


def features_of(raw):
    return feature(raw.astype(F32)).astype(BF)


def causal_mask():
    row = lax.broadcasted_iota(jnp.int32, (BLK, BLK), 0)
    col = lax.broadcasted_iota(jnp.int32, (BLK, BLK), 1)
    return row >= col


def state_of(ref, head):
    low, high = 2 * head, 2 * head + 1
    matrix = jnp.concatenate([ref[low, :HALF], ref[high, :HALF]], axis=0)
    return matrix, ref[low, HALF : HALF + 1]


def put_state(ref, head, matrix, vector):
    tail = jnp.broadcast_to(vector, (8, DH))
    for half in range(2):
        ref[2 * head + half, :HALF] = matrix[half * HALF : (half + 1) * HALF]
        ref[2 * head + half, HALF:ROWS] = tail


def call(body, grid, ins, outs, scratch=(), aliases=()):
    run = pl.pallas_call(
        body,
        grid_spec=pltpu.PrefetchScalarGridSpec(
            num_scalar_prefetch=1,
            grid=grid,
            in_specs=[pl.BlockSpec(*spec[:2], memory_space=(spec[2:] or (None,))[0]) for spec in ins],
            out_specs=[pl.BlockSpec(spec[0], spec[1]) for spec in outs],
            scratch_shapes=list(scratch),
        ),
        out_shape=[pltpu.HBM(spec[2], spec[3]) for spec in outs],
        input_output_aliases=dict(aliases),
        compiler_params=PARAMS,
    )

    return run


def kept_out(*arrays):
    return [pltpu.with_memory_space_constraint(array, pltpu.HBM) for array in arrays]


def put_pair(ref, head, core, mine, other):
    cols = pl.ds(pl.multiple_of((2 * head + core) * DH, DH), DH)
    ref[head, core] = mine[:, cols]
    ref[head, 1 - core] = other[:, cols]


def local_body(place, k_ref, v_ref, k_other, v_other, keys, values, sum_ref, first_ref):
    for head in range(keys.shape[0]):
        put_pair(keys, head, place[0], k_ref, k_other)
        put_pair(values, head, place[0], v_ref, v_other)
    for head in range(keys.shape[0]):
        feats = [features_of(keys[head, block]) for block in range(2)]
        states = [dot(feats[block], values[head, block], TN) for block in range(2)]
        norms = [jnp.sum(feat.astype(F32), axis=0, keepdims=True) for feat in feats]
        put_state(first_ref, head, states[0], norms[0])
        put_state(sum_ref, head, states[0] + states[1], norms[0] + norms[1])


def scan_body(place, in_ref, out_ref):
    count = in_ref.shape[0]
    so_far = jnp.zeros(in_ref.shape[1:], F32)
    for position in range(count):
        out_ref[position] = so_far
        so_far = so_far + in_ref[position]


def back_scan_body(place, in_ref, out_ref):
    count = in_ref.shape[0]
    so_far = jnp.zeros(in_ref.shape[1:], F32)
    for position in range(count - 1, -1, -1):
        out_ref[position] = so_far
        so_far = so_far + in_ref[position]


def total_body(place, in_ref, keep_ref, send_ref):
    total = in_ref[0].astype(F32)
    for position in range(1, in_ref.shape[0]):
        total = total + in_ref[position].astype(F32)
    low, high = total[:8], total[8:]
    keep_ref[...] = jnp.where(place[0] == 0, low, high)
    send_ref[...] = jnp.where(place[0] == 0, high, low)


def attn_grad_body(count, ahead_of, place, *refs):
    *og_refs, w_ref, out_ref, tokens, arrived = refs
    copies = []
    for position, ref in enumerate(og_refs):
        here = tokens.at[pl.ds(position * BLK, BLK)]
        copies.append(pltpu.make_async_copy(ref, here, arrived.at[position]))
        copies[-1].start()
    batch = (len(og_refs) + 1) // 2
    for first in range(0, len(og_refs), batch):
        last = min(first + batch, len(og_refs))
        for copy in copies[first:last]:
            copy.wait()
        part = dot(tokens[first * BLK : last * BLK], w_ref[...], NT).astype(BF)
        for position in range(first, last):
            start = (position - first) * BLK
            out_ref[lax.rem(place[3] + ahead_of[position], count)] = part[start : start + BLK]


def last_grad_body(place, low_ref, high_ref, w_ref, _, out_ref):
    rows = jnp.concatenate([low_ref[...], high_ref[...]], axis=0)
    out_ref[0] = dot(rows, w_ref[...], NT).astype(BF)


def forward_body(
    place,
    q_ref,
    q_other,
    keys,
    values,
    in_ref,
    first_ref,
    queries,
    copy_ref,
    att_ref,
    o_ref,
    den_ref,
):
    copy_ref[...] = in_ref[...]
    causal = causal_mask()
    for head in range(keys.shape[0]):
        put_pair(queries, head, place[0], q_ref, q_other)
    for head in range(keys.shape[0]):
        state, norm = state_of(in_ref, head)
        extra, extra_norm = state_of(first_ref, head)
        for block in range(2):
            if block == 1:
                state, norm = state + extra, norm + extra_norm
            q_feat = features_of(queries[head, block])
            k_feat = features_of(keys[head, block])
            scores = jnp.where(causal, dot(q_feat, k_feat, NT), 0.0)
            den = jnp.sum(scores, axis=1, keepdims=True) + jnp.sum(
                q_feat.astype(F32) * norm, axis=1, keepdims=True
            )
            high, low = split(state)
            out = (
                dot(scores.astype(BF), values[head, block], NN)
                + dot(q_feat, high, NN)
                + dot(q_feat, low, NN)
            ) / den
            att_ref[head, block * BLK : (block + 1) * BLK] = out.astype(BF)
            o_ref[head, block] = out
            den_ref[head, block] = jnp.broadcast_to(den, (BLK, DH))


def scaled_body(
    place,
    queries,
    o_ref,
    den_ref,
    grad_ref,
    grad_other,
    g_ref,
    r_ref,
    sum_ref,
    last_ref,
    grads,
):
    me = place[0]
    cols = pl.ds(pl.multiple_of(me * DH, DH), DH)
    for head in range(queries.shape[0]):
        grads[head, me] = grad_ref[head, :, cols]
        grads[head, 1 - me] = grad_other[head, :, cols]
    for head in range(queries.shape[0]):
        sums, norms = [], []
        for block in range(2):
            q_feat = features_of(queries[head, block])
            scaled = grads[head, block].astype(F32) / den_ref[head, block]
            g_ref[head, block] = scaled
            residue = -jnp.sum(scaled * o_ref[head, block], axis=1, keepdims=True)
            r_ref[head, block] = jnp.broadcast_to(residue, (BLK, DH))
            high, low = split(scaled)
            sums.append(dot(q_feat, high, TN) + dot(q_feat, low, TN))
            norms.append(jnp.sum(residue * q_feat.astype(F32), axis=0, keepdims=True))
        put_state(last_ref, head, sums[1], norms[1])
        put_state(sum_ref, head, sums[0] + sums[1], norms[0] + norms[1])


def backward_body(
    place,
    queries,
    keys,
    values,
    in_ref,
    first_ref,
    g_ref,
    r_ref,
    later_ref,
    last_ref,
    keep_ref,
    send_ref,
    held,
):
    me = place[0]
    causal = causal_mask()
    for head in range(keys.shape[0]):
        state0, norm0 = state_of(in_ref, head)
        extra, extra_norm = state_of(first_ref, head)
        grad1, weight1 = state_of(later_ref, head)
        after, after_norm = state_of(last_ref, head)
        states = (state0, state0 + extra)
        norms = (norm0, norm0 + extra_norm)
        grads = (grad1 + after, grad1)
        weights = (weight1 + after_norm, weight1)
        for block in range(2):
            q_raw = queries[head, block].astype(F32)
            k_raw = keys[head, block].astype(F32)
            v_full = values[head, block]
            q_feat, k_feat = feature(q_raw).astype(BF), feature(k_raw).astype(BF)
            scaled, residue = g_ref[head, block], r_ref[head, block]
            g_high, g_low = split(scaled)
            s_high, s_low = split(states[block])
            grad_high, grad_low = split(grads[block])
            scores = jnp.where(causal, dot(q_feat, k_feat, NT), 0.0).astype(BF)
            mixed = jnp.where(causal, dot(g_high, v_full, NT) + residue, 0.0).astype(BF)
            q_grad = (
                dot(mixed, k_feat, NN)
                + (dot(g_high, s_high, NT) + dot(g_high, s_low, NT) + dot(g_low, s_high, NT))
                + residue * norms[block]
            )
            k_grad = (
                dot(mixed, q_feat, TN)
                + (dot(v_full, grad_high, NT) + dot(v_full, grad_low, NT))
                + weights[block]
            )
            v_grad = dot(scores, g_high, TN) + (
                dot(k_feat, grad_high, NN) + dot(k_feat, grad_low, NN)
            )
            held[block, head, 0] = (q_grad * feature_slope(q_raw)).astype(BF)
            held[block, head, 1] = (k_grad * feature_slope(k_raw)).astype(BF)
            held[block, head, 2] = v_grad.astype(BF)
    keep_ref[...] = held[me]
    send_ref[...] = held[1 - me]


def merge_body(place, keep_ref, back_ref, q_ref, k_ref, v_ref):
    for head in range(keep_ref.shape[0]):
        mine = pl.ds(pl.multiple_of((2 * head + place[0]) * DH, DH), DH)
        other = pl.ds(pl.multiple_of((2 * head + 1 - place[0]) * DH, DH), DH)
        for part, ref in enumerate((q_ref, k_ref, v_ref)):
            ref[:, mine] = keep_ref[head, part]
            ref[:, other] = back_ref[head, part]


def weight_body(steps, count, place, mine_ref, other_ref, *refs):
    *og_refs, send_ref, keep_ref, heads = refs
    left = pl.ds(pl.multiple_of(place[0] * DH, DH), DH)
    right = pl.ds(pl.multiple_of((1 - place[0]) * DH, DH), DH)

    @pl.when(pl.program_id(0) == 0)
    def _():
        for ahead in range(count):
            source = lax.rem(place[3] + ahead, count)
            heads[ahead * BLK : (ahead + 1) * BLK, left] = mine_ref[source]
            heads[ahead * BLK : (ahead + 1) * BLK, right] = other_ref[source]

    right_side = jnp.concatenate([ref[...] for ref in og_refs], axis=0)
    part = dot(heads[...], right_side, TN)

    @pl.when(pl.program_id(0) < steps)
    def _():
        send_ref[...] = part

    @pl.when(pl.program_id(0) >= steps)
    def _():
        keep_ref[...] = part


def on_device(nx, ny, nz, queries, keys, values, out_grad, out_weight):
    chips = nx * ny
    tok, width = queries.shape[1:]
    pairs = width // (2 * DH)
    model = out_grad.shape[2]
    half = model // 2
    me = lax.axis_index("c")
    place = jnp.stack([lax.axis_index(name) for name in ("c", "x", "y", "z")]).astype(jnp.int32)
    q_in, k_in, v_in, og = (
        part.reshape(tok, part.shape[2]) for part in (queries, keys, values, out_grad)
    )
    swap = functools.partial(lax.ppermute, axis_name="c", perm=[(0, 1), (1, 0)])
    plane = ("x", "y")

    def from_ahead(piece, axis, size, ahead):
        return lax.ppermute(piece, axis, [((i + ahead) % size, i) for i in range(size)])

    k_other, v_other, q_other = swap(k_in), swap(v_in), swap(q_in)

    def both_ways(up, down):
        return from_ahead(up, "z", nz, 1), from_ahead(down, "z", nz, -1)

    og_1, og_7 = both_ways(og, og)
    og_2, og_6 = both_ways(og_1, og_7)
    og_3, og_5 = both_ways(og_2, og_6)
    low, high = both_ways(og_3[: tok // 2], og_5[tok // 2 :])
    og_all = kept_out(og, og_1, og_2, og_3, low, high, og_5, og_6, og_7)

    heads = 2
    grid = (pairs // heads,)
    lead = lambda j, p: (j, 0, 0)
    lead4 = lambda j, p: (j, 0, 0, 0)
    state_spec = ((2 * heads, ROWS, DH), lead)
    state_out = (*state_spec, (2 * pairs, ROWS, DH), F32)
    pair_spec = ((heads, 2, tok, DH), lead4)
    pair_out = (*pair_spec, (pairs, 2, tok, DH), F32)
    both_out = (*pair_spec, (pairs, 2, tok, DH), BF)
    head_spec = ((tok, 2 * heads * DH), lambda j, p: (0, j))
    whole = lambda *shape: (shape, lambda j, p: (0,) * len(shape))

    keys_all, values_all, local_sum, first = call(
        local_body, grid, [head_spec] * 4, [both_out, both_out, state_out, state_out]
    )(place, *kept_out(k_in, v_in), k_other, v_other)
    keys_all, values_all, first = kept_out(keys_all, values_all, first)

    out_weight = lax.optimization_barrier((out_weight, local_sum))[0]

    def fetched(piece, axis, size):
        return [from_ahead(piece, axis, size, ahead) for ahead in range(1, size)]

    def gathered(piece, fetched_parts, start):
        size = len(fetched_parts) + 1
        whole = jnp.broadcast_to(piece[None], (size, *piece.shape))
        for ahead, part in enumerate(fetched_parts, start=1):
            place = lax.rem(start + ahead, size)
            whole = lax.dynamic_update_index_in_dim(whole, part, place, 0)
        return whole

    row_group = gathered(out_weight, fetched(out_weight, "y", ny), lax.axis_index("y"))
    row_groups = fetched(row_group, "x", nx)

    parts = lax.all_to_all(local_sum, plane, 0, 0, tiled=True)
    earlier = call(
        scan_body,
        (1,),
        [whole(chips, ROWS, DH)],
        [(*whole(chips, ROWS, DH), (chips, ROWS, DH), F32)],
    )(place, parts)[0]
    earlier = lax.all_to_all(earlier, plane, 0, 0, tiled=True)
    queries_all, earlier, attended, outputs, dens = call(
        forward_body,
        grid,
        [head_spec] * 2 + [pair_spec] * 2 + [state_spec] * 2,
        [both_out, state_out]
        + [((heads, 2 * tok, DH), lead, (pairs, 2 * tok, DH), BF), pair_out, pair_out],
    )(place, *kept_out(q_in), q_other, keys_all, values_all, earlier, first)
    row_groups = lax.optimization_barrier((row_groups, attended))[0]
    rows_mine = gathered(row_group, row_groups, lax.axis_index("x")).reshape(chips, 8, model)
    rows_other = swap(rows_mine)
    rows = jnp.where(
        me == 0,
        jnp.stack([rows_mine, rows_other], axis=1),
        jnp.stack([rows_other, rows_mine], axis=1),
    ).reshape(2 * DH, model)
    att_mine = lax.all_to_all(attended, "z", 0, 0, tiled=True)
    att_other = swap(att_mine)

    ahead_of = [*range(nz // 2), *range(nz // 2 + 1, nz)]
    early = [part for part in og_all if part.shape[0] == tok]
    grads_shape = (nz, tok, 2 * DH)
    attn_grad = call(
        functools.partial(attn_grad_body, nz, ahead_of),
        (1,),
        [(None, None, pl.ANY)] * len(early) + [whole(2 * DH, model)],
        [(*whole(*grads_shape), grads_shape, BF)],
        [
            pltpu.VMEM((len(early) * tok, model), BF),
            pltpu.SemaphoreType.DMA((len(early),)),
        ],
    )(place, *early, rows)[0]
    attn_grad = call(
        last_grad_body,
        (1,),
        [whole(tok // 2, model)] * 2 + [whole(2 * DH, model), (None, None, pl.ANY)],
        [
            (
                (1, tok, 2 * DH),
                lambda j, p: (lax.rem(p[3] + nz // 2, nz), 0, 0),
                grads_shape,
                BF,
            )
        ],
        aliases={4: 0},
    )(place, *kept_out(low, high), rows, *kept_out(attn_grad))[0]
    attn_grad, att_mine = lax.optimization_barrier((attn_grad, att_mine))
    grad_mine = lax.all_to_all(attn_grad, "z", 0, 0, tiled=True)

    steps = 2
    cols = half // steps
    att_spec = ((nz, tok, DH), lambda j, p: (0, p[0], 0))
    og_col = lambda j, p: (0, jnp.where(j < steps, 1 - p[0], p[0]) * steps + lax.rem(j, steps))
    moved, kept = call(
        functools.partial(weight_body, steps, nz),
        (2 * steps,),
        [att_spec] * 2 + [((part.shape[0], cols), og_col) for part in og_all],
        [
            ((2 * DH, cols), lambda j, p: (0, jnp.minimum(j, steps - 1)), (2 * DH, half), F32),
            ((2 * DH, cols), lambda j, p: (0, jnp.maximum(j - steps, 0)), (2 * DH, half), F32),
        ],
        [pltpu.VMEM((nz * tok, 2 * DH), BF)],
    )(place, att_mine, att_other, *og_all)
    grad_mine, moved, kept = lax.optimization_barrier((grad_mine, moved, kept))
    grad_other = swap(grad_mine)
    got = swap(moved)

    grad_spec = ((heads, tok, 2 * DH), lead)
    scaled, residue, grad_sum, last = call(
        scaled_body,
        grid,
        [pair_spec] * 3 + [grad_spec] * 2,
        [pair_out, pair_out, state_out, state_out],
        [pltpu.VMEM((heads, 2, tok, DH), BF)],
    )(
        place,
        *kept_out(queries_all, outputs, dens),
        *(grad_mine, grad_other),
    )
    parts = lax.all_to_all(grad_sum, plane, 0, 0, tiled=True)
    later = call(
        back_scan_body,
        (1,),
        [whole(chips, ROWS, DH)],
        [(*whole(chips, ROWS, DH), (chips, ROWS, DH), F32)],
    )(place, parts)[0]
    later = lax.all_to_all(later, plane, 0, 0, tiled=True)
    shares = (kept + got).astype(BF).reshape(chips, 2 * DH // chips, half)
    later, shares = lax.optimization_barrier((later, shares))
    shares = lax.all_to_all(shares, plane, 0, 0, tiled=True)
    grad_out = ((heads, 3, tok, DH), lead4, (pairs, 3, tok, DH), BF)
    keep, send = call(
        backward_body,
        grid,
        [pair_spec] * 3
        + [state_spec, state_spec, pair_spec, pair_spec, state_spec, state_spec],
        [grad_out] * 2,
        [pltpu.VMEM((2, heads, 3, tok, DH), BF)],
    )(
        place,
        *kept_out(queries_all, keys_all, values_all, earlier, first, scaled, residue),
        later,
        *kept_out(last),
    )
    send, shares = lax.optimization_barrier((send, shares))
    back = swap(send)
    weight_kept, weight_moved = call(
        total_body,
        (1,),
        [whole(*shares.shape)],
        [(*whole(8, half), (8, half), F32)] * 2,
    )(place, shares)
    weight_got = swap(weight_moved)
    weight_grad = jnp.where(
        me == 0,
        jnp.concatenate([weight_kept, weight_got], axis=1),
        jnp.concatenate([weight_got, weight_kept], axis=1),
    )
    grads = call(
        merge_body,
        (1,),
        [whole(pairs, 3, tok, DH)] * 2,
        [(*whole(tok, width), (tok, width), BF)] * 3,
    )(place, *kept_out(keep), back)
    return (*(grad.reshape(1, tok, width) for grad in grads), weight_grad)


def solution(mesh):
    nz, nx, ny = mesh.shape["dp"], 4, mesh.shape["seq"] // 8
    grid = Mesh(mesh.devices.reshape(nz, nx, ny, 2), ("z", "x", "y", "c"))
    tokens = P("z", ("x", "y", "c"), None)
    weights = P(("z", "x", "y", "c"), None)
    return jax.shard_map(
        functools.partial(on_device, nx, ny, nz),
        mesh=grid,
        in_specs=(tokens, tokens, tokens, tokens, weights),
        out_specs=(tokens, tokens, tokens, weights),
        check_vma=False,
    )
```

```python
import functools

import jax
import jax.numpy as jnp
from jax import lax
from jax.experimental import pallas as pl
from jax.experimental.pallas import tpu as pltpu
from jax.sharding import Mesh, PartitionSpec as P

DH = 128
BLK = 128
BF = jnp.bfloat16
F32 = jnp.float32
NN = (((1,), (0,)), ((), ()))
NT = (((1,), (1,)), ((), ()))
TN = (((0,), (0,)), ((), ()))
HALF = DH // 2
ROWS = HALF + 8
PARAMS = pltpu.CompilerParams(vmem_limit_bytes=24 * 1024 * 1024)


def dot(left, right, dims):
    return lax.dot_general(left, right, dims, preferred_element_type=F32)


def split(wide):
    high = wide.astype(BF)
    return high, (wide - high.astype(F32)).astype(BF)


def feature(raw):
    return jnp.where(raw > 0, raw + 1.0, jnp.exp(jnp.minimum(raw, 0.0)))


def feature_slope(raw):
    return jnp.where(raw > 0, 1.0, jnp.exp(jnp.minimum(raw, 0.0)))


def features_of(raw):
    return feature(raw.astype(F32)).astype(BF)


def causal_mask():
    row = lax.broadcasted_iota(jnp.int32, (BLK, BLK), 0)
    col = lax.broadcasted_iota(jnp.int32, (BLK, BLK), 1)
    return row >= col


def state_of(ref, head):
    low, high = 2 * head, 2 * head + 1
    matrix = jnp.concatenate([ref[low, :HALF], ref[high, :HALF]], axis=0)
    return matrix, ref[low, HALF : HALF + 1]


def put_state(ref, head, matrix, vector):
    tail = jnp.broadcast_to(vector, (8, DH))
    for half in range(2):
        ref[2 * head + half, :HALF] = matrix[half * HALF : (half + 1) * HALF]
        ref[2 * head + half, HALF:ROWS] = tail


def call(body, grid, ins, outs, scratch=(), aliases=()):
    run = pl.pallas_call(
        body,
        grid_spec=pltpu.PrefetchScalarGridSpec(
            num_scalar_prefetch=1,
            grid=grid,
            in_specs=[pl.BlockSpec(*spec[:2], memory_space=(spec[2:] or (None,))[0]) for spec in ins],
            out_specs=[pl.BlockSpec(spec[0], spec[1]) for spec in outs],
            scratch_shapes=list(scratch),
        ),
        out_shape=[pltpu.HBM(spec[2], spec[3]) for spec in outs],
        input_output_aliases=dict(aliases),
        compiler_params=PARAMS,
    )

    return run


def kept_out(*arrays):
    return [pltpu.with_memory_space_constraint(array, pltpu.HBM) for array in arrays]


def put_pair(ref, head, core, mine, other):
    cols = pl.ds(pl.multiple_of((2 * head + core) * DH, DH), DH)
    ref[head, core] = mine[:, cols]
    ref[head, 1 - core] = other[:, cols]


def local_body(place, k_ref, v_ref, k_other, v_other, keys, values, sum_ref, first_ref):
    for head in range(keys.shape[0]):
        put_pair(keys, head, place[0], k_ref, k_other)
        put_pair(values, head, place[0], v_ref, v_other)
    for head in range(keys.shape[0]):
        feats = [features_of(keys[head, block]) for block in range(2)]
        states = [dot(feats[block], values[head, block], TN) for block in range(2)]
        norms = [jnp.sum(feat.astype(F32), axis=0, keepdims=True) for feat in feats]
        put_state(first_ref, head, states[0], norms[0])
        put_state(sum_ref, head, states[0] + states[1], norms[0] + norms[1])


def scan_body(place, in_ref, out_ref):
    count = in_ref.shape[0]
    so_far = jnp.zeros(in_ref.shape[1:], F32)
    for position in range(count):
        out_ref[position] = so_far
        so_far = so_far + in_ref[position]


def back_scan_body(place, in_ref, out_ref):
    count = in_ref.shape[0]
    so_far = jnp.zeros(in_ref.shape[1:], F32)
    for position in range(count - 1, -1, -1):
        out_ref[position] = so_far
        so_far = so_far + in_ref[position]


def total_body(place, in_ref, keep_ref, send_ref):
    total = in_ref[0].astype(F32)
    for position in range(1, in_ref.shape[0]):
        total = total + in_ref[position].astype(F32)
    low, high = total[:8], total[8:]
    keep_ref[...] = jnp.where(place[0] == 0, low, high)
    send_ref[...] = jnp.where(place[0] == 0, high, low)


def attn_grad_body(count, ahead_of, place, *refs):
    *og_refs, w_ref, out_ref, tokens, arrived = refs
    copies = []
    for position, ref in enumerate(og_refs):
        here = tokens.at[pl.ds(position * BLK, BLK)]
        copies.append(pltpu.make_async_copy(ref, here, arrived.at[position]))
        copies[-1].start()
    batch = (len(og_refs) + 1) // 2
    for first in range(0, len(og_refs), batch):
        last = min(first + batch, len(og_refs))
        for copy in copies[first:last]:
            copy.wait()
        part = dot(tokens[first * BLK : last * BLK], w_ref[...], NT).astype(BF)
        for position in range(first, last):
            start = (position - first) * BLK
            out_ref[lax.rem(place[3] + ahead_of[position], count)] = part[start : start + BLK]


def last_grad_body(place, low_ref, high_ref, w_ref, _, out_ref):
    rows = jnp.concatenate([low_ref[...], high_ref[...]], axis=0)
    out_ref[0] = dot(rows, w_ref[...], NT).astype(BF)


def forward_body(
    place,
    q_ref,
    q_other,
    keys,
    values,
    in_ref,
    first_ref,
    queries,
    copy_ref,
    att_ref,
    o_ref,
    den_ref,
):
    copy_ref[...] = in_ref[...]
    causal = causal_mask()
    for head in range(keys.shape[0]):
        put_pair(queries, head, place[0], q_ref, q_other)
    for head in range(keys.shape[0]):
        state, norm = state_of(in_ref, head)
        extra, extra_norm = state_of(first_ref, head)
        for block in range(2):
            if block == 1:
                state, norm = state + extra, norm + extra_norm
            q_feat = features_of(queries[head, block])
            k_feat = features_of(keys[head, block])
            scores = jnp.where(causal, dot(q_feat, k_feat, NT), 0.0)
            den = jnp.sum(scores, axis=1, keepdims=True) + jnp.sum(
                q_feat.astype(F32) * norm, axis=1, keepdims=True
            )
            high, low = split(state)
            out = (
                dot(scores.astype(BF), values[head, block], NN)
                + dot(q_feat, high, NN)
                + dot(q_feat, low, NN)
            ) / den
            att_ref[head, block * BLK : (block + 1) * BLK] = out.astype(BF)
            o_ref[head, block] = out
            den_ref[head, block] = jnp.broadcast_to(den, (BLK, DH))


def scaled_body(
    place,
    queries,
    o_ref,
    den_ref,
    grad_ref,
    grad_other,
    g_ref,
    r_ref,
    sum_ref,
    last_ref,
    grads,
):
    me = place[0]
    cols = pl.ds(pl.multiple_of(me * DH, DH), DH)
    for head in range(queries.shape[0]):
        grads[head, me] = grad_ref[head, :, cols]
        grads[head, 1 - me] = grad_other[head, :, cols]
    for head in range(queries.shape[0]):
        sums, norms = [], []
        for block in range(2):
            q_feat = features_of(queries[head, block])
            scaled = grads[head, block].astype(F32) / den_ref[head, block]
            g_ref[head, block] = scaled
            residue = -jnp.sum(scaled * o_ref[head, block], axis=1, keepdims=True)
            r_ref[head, block] = jnp.broadcast_to(residue, (BLK, DH))
            high, low = split(scaled)
            sums.append(dot(q_feat, high, TN) + dot(q_feat, low, TN))
            norms.append(jnp.sum(residue * q_feat.astype(F32), axis=0, keepdims=True))
        put_state(last_ref, head, sums[1], norms[1])
        put_state(sum_ref, head, sums[0] + sums[1], norms[0] + norms[1])


def backward_body(
    place,
    queries,
    keys,
    values,
    in_ref,
    first_ref,
    g_ref,
    r_ref,
    later_ref,
    last_ref,
    keep_ref,
    send_ref,
    held,
):
    me = place[0]
    causal = causal_mask()
    for head in range(keys.shape[0]):
        state0, norm0 = state_of(in_ref, head)
        extra, extra_norm = state_of(first_ref, head)
        grad1, weight1 = state_of(later_ref, head)
        after, after_norm = state_of(last_ref, head)
        states = (state0, state0 + extra)
        norms = (norm0, norm0 + extra_norm)
        grads = (grad1 + after, grad1)
        weights = (weight1 + after_norm, weight1)
        for block in range(2):
            q_raw = queries[head, block].astype(F32)
            k_raw = keys[head, block].astype(F32)
            v_full = values[head, block]
            q_feat, k_feat = feature(q_raw).astype(BF), feature(k_raw).astype(BF)
            scaled, residue = g_ref[head, block], r_ref[head, block]
            g_high, g_low = split(scaled)
            s_high, s_low = split(states[block])
            grad_high, grad_low = split(grads[block])
            scores = jnp.where(causal, dot(q_feat, k_feat, NT), 0.0).astype(BF)
            mixed = jnp.where(causal, dot(g_high, v_full, NT) + residue, 0.0).astype(BF)
            q_grad = (
                dot(mixed, k_feat, NN)
                + (dot(g_high, s_high, NT) + dot(g_high, s_low, NT) + dot(g_low, s_high, NT))
                + residue * norms[block]
            )
            k_grad = (
                dot(mixed, q_feat, TN)
                + (dot(v_full, grad_high, NT) + dot(v_full, grad_low, NT))
                + weights[block]
            )
            v_grad = dot(scores, g_high, TN) + (
                dot(k_feat, grad_high, NN) + dot(k_feat, grad_low, NN)
            )
            held[block, head, 0] = (q_grad * feature_slope(q_raw)).astype(BF)
            held[block, head, 1] = (k_grad * feature_slope(k_raw)).astype(BF)
            held[block, head, 2] = v_grad.astype(BF)
    keep_ref[...] = held[me]
    send_ref[...] = held[1 - me]


def merge_body(place, keep_ref, back_ref, q_ref, k_ref, v_ref):
    for head in range(keep_ref.shape[0]):
        mine = pl.ds(pl.multiple_of((2 * head + place[0]) * DH, DH), DH)
        other = pl.ds(pl.multiple_of((2 * head + 1 - place[0]) * DH, DH), DH)
        for part, ref in enumerate((q_ref, k_ref, v_ref)):
            ref[:, mine] = keep_ref[head, part]
            ref[:, other] = back_ref[head, part]


def weight_body(steps, count, place, mine_ref, other_ref, *refs):
    *og_refs, send_ref, keep_ref, heads = refs
    left = pl.ds(pl.multiple_of(place[0] * DH, DH), DH)
    right = pl.ds(pl.multiple_of((1 - place[0]) * DH, DH), DH)

    @pl.when(pl.program_id(0) == 0)
    def _():
        for ahead in range(count):
            source = lax.rem(place[3] + ahead, count)
            heads[ahead * BLK : (ahead + 1) * BLK, left] = mine_ref[source]
            heads[ahead * BLK : (ahead + 1) * BLK, right] = other_ref[source]

    right_side = jnp.concatenate([ref[...] for ref in og_refs], axis=0)
    part = dot(heads[...], right_side, TN)

    @pl.when(pl.program_id(0) < steps)
    def _():
        send_ref[...] = part

    @pl.when(pl.program_id(0) >= steps)
    def _():
        keep_ref[...] = part


def on_device(nx, ny, nz, queries, keys, values, out_grad, out_weight):
    chips = nx * ny
    tok, width = queries.shape[1:]
    pairs = width // (2 * DH)
    model = out_grad.shape[2]
    half = model // 2
    me = lax.axis_index("c")
    place = jnp.stack([lax.axis_index(name) for name in ("c", "x", "y", "z")]).astype(jnp.int32)
    q_in, k_in, v_in, og = (
        part.reshape(tok, part.shape[2]) for part in (queries, keys, values, out_grad)
    )
    swap = functools.partial(lax.ppermute, axis_name="c", perm=[(0, 1), (1, 0)])
    plane = ("x", "y")

    def from_ahead(piece, axis, size, ahead):
        return lax.ppermute(piece, axis, [((i + ahead) % size, i) for i in range(size)])

    k_other, v_other, q_other = swap(k_in), swap(v_in), swap(q_in)

    def both_ways(up, down):
        return from_ahead(up, "z", nz, 1), from_ahead(down, "z", nz, -1)

    og_1, og_7 = both_ways(og, og)
    og_2, og_6 = both_ways(og_1, og_7)
    og_3, og_5 = both_ways(og_2, og_6)
    low, high = both_ways(og_3[: tok // 2], og_5[tok // 2 :])
    og_all = kept_out(og, og_1, og_2, og_3, low, high, og_5, og_6, og_7)

    heads = 4
    grid = (pairs // heads,)
    lead = lambda j, p: (j, 0, 0)
    lead4 = lambda j, p: (j, 0, 0, 0)
    state_spec = ((2 * heads, ROWS, DH), lead)
    state_out = (*state_spec, (2 * pairs, ROWS, DH), F32)
    pair_spec = ((heads, 2, tok, DH), lead4)
    pair_out = (*pair_spec, (pairs, 2, tok, DH), F32)
    both_out = (*pair_spec, (pairs, 2, tok, DH), BF)
    head_spec = ((tok, 2 * heads * DH), lambda j, p: (0, j))
    whole = lambda *shape: (shape, lambda j, p: (0,) * len(shape))

    keys_all, values_all, local_sum, first = call(
        local_body, grid, [head_spec] * 4, [both_out, both_out, state_out, state_out]
    )(place, *kept_out(k_in, v_in), k_other, v_other)
    keys_all, values_all, first = kept_out(keys_all, values_all, first)

    out_weight = lax.optimization_barrier((out_weight, local_sum))[0]

    def fetched(piece, axis, size):
        return [from_ahead(piece, axis, size, ahead) for ahead in range(1, size)]

    def gathered(piece, fetched_parts, start):
        size = len(fetched_parts) + 1
        whole = jnp.broadcast_to(piece[None], (size, *piece.shape))
        for ahead, part in enumerate(fetched_parts, start=1):
            place = lax.rem(start + ahead, size)
            whole = lax.dynamic_update_index_in_dim(whole, part, place, 0)
        return whole

    row_group = gathered(out_weight, fetched(out_weight, "y", ny), lax.axis_index("y"))
    row_groups = fetched(row_group, "x", nx)

    parts = lax.all_to_all(local_sum, plane, 0, 0, tiled=True)
    earlier = call(
        scan_body,
        (1,),
        [whole(chips, ROWS, DH)],
        [(*whole(chips, ROWS, DH), (chips, ROWS, DH), F32)],
    )(place, parts)[0]
    earlier = lax.all_to_all(earlier, plane, 0, 0, tiled=True)
    queries_all, earlier, attended, outputs, dens = call(
        forward_body,
        grid,
        [head_spec] * 2 + [pair_spec] * 2 + [state_spec] * 2,
        [both_out, state_out]
        + [((heads, 2 * tok, DH), lead, (pairs, 2 * tok, DH), BF), pair_out, pair_out],
    )(place, *kept_out(q_in), q_other, keys_all, values_all, earlier, first)
    row_groups = lax.optimization_barrier((row_groups, attended))[0]
    rows_mine = gathered(row_group, row_groups, lax.axis_index("x")).reshape(chips, 8, model)
    rows_other = swap(rows_mine)
    rows = jnp.where(
        me == 0,
        jnp.stack([rows_mine, rows_other], axis=1),
        jnp.stack([rows_other, rows_mine], axis=1),
    ).reshape(2 * DH, model)
    att_mine = lax.all_to_all(attended, "z", 0, 0, tiled=True)
    att_other = swap(att_mine)

    ahead_of = [*range(nz // 2), *range(nz // 2 + 1, nz)]
    early = [part for part in og_all if part.shape[0] == tok]
    grads_shape = (nz, tok, 2 * DH)
    attn_grad = call(
        functools.partial(attn_grad_body, nz, ahead_of),
        (1,),
        [(None, None, pl.ANY)] * len(early) + [whole(2 * DH, model)],
        [(*whole(*grads_shape), grads_shape, BF)],
        [
            pltpu.VMEM((len(early) * tok, model), BF),
            pltpu.SemaphoreType.DMA((len(early),)),
        ],
    )(place, *early, rows)[0]
    attn_grad = call(
        last_grad_body,
        (1,),
        [whole(tok // 2, model)] * 2 + [whole(2 * DH, model), (None, None, pl.ANY)],
        [
            (
                (1, tok, 2 * DH),
                lambda j, p: (lax.rem(p[3] + nz // 2, nz), 0, 0),
                grads_shape,
                BF,
            )
        ],
        aliases={4: 0},
    )(place, *kept_out(low, high), rows, *kept_out(attn_grad))[0]
    attn_grad, att_mine = lax.optimization_barrier((attn_grad, att_mine))
    grad_mine = lax.all_to_all(attn_grad, "z", 0, 0, tiled=True)

    steps = 2
    cols = half // steps
    att_spec = ((nz, tok, DH), lambda j, p: (0, p[0], 0))
    og_col = lambda j, p: (0, jnp.where(j < steps, 1 - p[0], p[0]) * steps + lax.rem(j, steps))
    moved, kept = call(
        functools.partial(weight_body, steps, nz),
        (2 * steps,),
        [att_spec] * 2 + [((part.shape[0], cols), og_col) for part in og_all],
        [
            ((2 * DH, cols), lambda j, p: (0, jnp.minimum(j, steps - 1)), (2 * DH, half), F32),
            ((2 * DH, cols), lambda j, p: (0, jnp.maximum(j - steps, 0)), (2 * DH, half), F32),
        ],
        [pltpu.VMEM((nz * tok, 2 * DH), BF)],
    )(place, att_mine, att_other, *og_all)
    grad_mine, moved, kept = lax.optimization_barrier((grad_mine, moved, kept))
    grad_other = swap(grad_mine)
    got = swap(moved)

    grad_spec = ((heads, tok, 2 * DH), lead)
    scaled, residue, grad_sum, last = call(
        scaled_body,
        grid,
        [pair_spec] * 3 + [grad_spec] * 2,
        [pair_out, pair_out, state_out, state_out],
        [pltpu.VMEM((heads, 2, tok, DH), BF)],
    )(
        place,
        *kept_out(queries_all, outputs, dens),
        *(grad_mine, grad_other),
    )
    parts = lax.all_to_all(grad_sum, plane, 0, 0, tiled=True)
    later = call(
        back_scan_body,
        (1,),
        [whole(chips, ROWS, DH)],
        [(*whole(chips, ROWS, DH), (chips, ROWS, DH), F32)],
    )(place, parts)[0]
    later = lax.all_to_all(later, plane, 0, 0, tiled=True)
    shares = (kept + got).astype(BF).reshape(chips, 2 * DH // chips, half)
    later, shares = lax.optimization_barrier((later, shares))
    shares = lax.all_to_all(shares, plane, 0, 0, tiled=True)
    grad_out = ((heads, 3, tok, DH), lead4, (pairs, 3, tok, DH), BF)
    keep, send = call(
        backward_body,
        grid,
        [pair_spec] * 3
        + [state_spec, state_spec, pair_spec, pair_spec, state_spec, state_spec],
        [grad_out] * 2,
        [pltpu.VMEM((2, heads, 3, tok, DH), BF)],
    )(
        place,
        *kept_out(queries_all, keys_all, values_all, earlier, first, scaled, residue),
        later,
        *kept_out(last),
    )
    send, shares = lax.optimization_barrier((send, shares))
    back = swap(send)
    weight_kept, weight_moved = call(
        total_body,
        (1,),
        [whole(*shares.shape)],
        [(*whole(8, half), (8, half), F32)] * 2,
    )(place, shares)
    weight_got = swap(weight_moved)
    weight_grad = jnp.where(
        me == 0,
        jnp.concatenate([weight_kept, weight_got], axis=1),
        jnp.concatenate([weight_got, weight_kept], axis=1),
    )
    grads = call(
        merge_body,
        (1,),
        [whole(pairs, 3, tok, DH)] * 2,
        [(*whole(tok, width), (tok, width), BF)] * 3,
    )(place, *kept_out(keep), back)
    return (*(grad.reshape(1, tok, width) for grad in grads), weight_grad)


def solution(mesh):
    nz, nx, ny = mesh.shape["dp"], 4, mesh.shape["seq"] // 8
    grid = Mesh(mesh.devices.reshape(nz, nx, ny, 2), ("z", "x", "y", "c"))
    tokens = P("z", ("x", "y", "c"), None)
    weights = P(("z", "x", "y", "c"), None)
    return jax.shard_map(
        functools.partial(on_device, nx, ny, nz),
        mesh=grid,
        in_specs=(tokens, tokens, tokens, tokens, weights),
        out_specs=(tokens, tokens, tokens, weights),
        check_vma=False,
    )
```

```python
import functools

import jax
import jax.numpy as jnp
from jax import lax
from jax.experimental import pallas as pl
from jax.experimental.pallas import tpu as pltpu
from jax.sharding import Mesh, PartitionSpec as P

DH = 128
BLK = 128
BF = jnp.bfloat16
F32 = jnp.float32
NN = (((1,), (0,)), ((), ()))
NT = (((1,), (1,)), ((), ()))
TN = (((0,), (0,)), ((), ()))
HALF = DH // 2
ROWS = HALF + 8
PARAMS = pltpu.CompilerParams(vmem_limit_bytes=24 * 1024 * 1024)


def dot(left, right, dims):
    return lax.dot_general(left, right, dims, preferred_element_type=F32)


def split(wide):
    high = wide.astype(BF)
    return high, (wide - high.astype(F32)).astype(BF)


def feature(raw):
    return jnp.where(raw > 0, raw + 1.0, jnp.exp(jnp.minimum(raw, 0.0)))


def feature_slope(raw):
    return jnp.where(raw > 0, 1.0, jnp.exp(jnp.minimum(raw, 0.0)))


def features_of(raw):
    return feature(raw.astype(F32)).astype(BF)


def causal_mask():
    row = lax.broadcasted_iota(jnp.int32, (BLK, BLK), 0)
    col = lax.broadcasted_iota(jnp.int32, (BLK, BLK), 1)
    return row >= col


def state_of(ref, head):
    low, high = 2 * head, 2 * head + 1
    matrix = jnp.concatenate([ref[low, :HALF], ref[high, :HALF]], axis=0)
    return matrix, ref[low, HALF : HALF + 1]


def put_state(ref, head, matrix, vector):
    tail = jnp.broadcast_to(vector, (8, DH))
    for half in range(2):
        ref[2 * head + half, :HALF] = matrix[half * HALF : (half + 1) * HALF]
        ref[2 * head + half, HALF:ROWS] = tail


def call(body, grid, ins, outs, scratch=(), aliases=()):
    run = pl.pallas_call(
        body,
        grid_spec=pltpu.PrefetchScalarGridSpec(
            num_scalar_prefetch=1,
            grid=grid,
            in_specs=[pl.BlockSpec(*spec[:2], memory_space=(spec[2:] or (None,))[0]) for spec in ins],
            out_specs=[pl.BlockSpec(spec[0], spec[1]) for spec in outs],
            scratch_shapes=list(scratch),
        ),
        out_shape=[pltpu.HBM(spec[2], spec[3]) for spec in outs],
        input_output_aliases=dict(aliases),
        compiler_params=PARAMS,
    )

    return run


def kept_out(*arrays):
    return [pltpu.with_memory_space_constraint(array, pltpu.HBM) for array in arrays]


def put_pair(ref, head, core, mine, other):
    cols = pl.ds(pl.multiple_of((2 * head + core) * DH, DH), DH)
    ref[head, core] = mine[:, cols]
    ref[head, 1 - core] = other[:, cols]


def local_body(place, k_ref, v_ref, k_other, v_other, keys, values, sum_ref, first_ref):
    for head in range(keys.shape[0]):
        put_pair(keys, head, place[0], k_ref, k_other)
        put_pair(values, head, place[0], v_ref, v_other)
    for head in range(keys.shape[0]):
        feats = [features_of(keys[head, block]) for block in range(2)]
        states = [dot(feats[block], values[head, block], TN) for block in range(2)]
        norms = [jnp.sum(feat.astype(F32), axis=0, keepdims=True) for feat in feats]
        put_state(first_ref, head, states[0], norms[0])
        put_state(sum_ref, head, states[0] + states[1], norms[0] + norms[1])


def scan_body(place, in_ref, out_ref):
    count = in_ref.shape[0]
    so_far = jnp.zeros(in_ref.shape[1:], F32)
    for position in range(count):
        out_ref[position] = so_far
        so_far = so_far + in_ref[position]


def back_scan_body(place, in_ref, out_ref):
    count = in_ref.shape[0]
    so_far = jnp.zeros(in_ref.shape[1:], F32)
    for position in range(count - 1, -1, -1):
        out_ref[position] = so_far
        so_far = so_far + in_ref[position]


def total_body(place, in_ref, keep_ref, send_ref):
    total = in_ref[0].astype(F32)
    for position in range(1, in_ref.shape[0]):
        total = total + in_ref[position].astype(F32)
    low, high = total[:8], total[8:]
    keep_ref[...] = jnp.where(place[0] == 0, low, high)
    send_ref[...] = jnp.where(place[0] == 0, high, low)


def attn_grad_body(count, ahead_of, place, *refs):
    *og_refs, w_ref, out_ref, tokens, arrived = refs
    copies = []
    for position, ref in enumerate(og_refs):
        here = tokens.at[pl.ds(position * BLK, BLK)]
        copies.append(pltpu.make_async_copy(ref, here, arrived.at[position]))
        copies[-1].start()
    batch = (len(og_refs) + 1) // 2
    for first in range(0, len(og_refs), batch):
        last = min(first + batch, len(og_refs))
        for copy in copies[first:last]:
            copy.wait()
        part = dot(tokens[first * BLK : last * BLK], w_ref[...], NT).astype(BF)
        for position in range(first, last):
            start = (position - first) * BLK
            out_ref[lax.rem(place[3] + ahead_of[position], count)] = part[start : start + BLK]


def last_grad_body(place, low_ref, high_ref, w_ref, _, out_ref):
    rows = jnp.concatenate([low_ref[...], high_ref[...]], axis=0)
    out_ref[0] = dot(rows, w_ref[...], NT).astype(BF)


def forward_body(
    place,
    q_ref,
    q_other,
    keys,
    values,
    in_ref,
    first_ref,
    queries,
    copy_ref,
    att_ref,
    o_ref,
    den_ref,
):
    copy_ref[...] = in_ref[...]
    causal = causal_mask()
    for head in range(keys.shape[0]):
        put_pair(queries, head, place[0], q_ref, q_other)
    for head in range(keys.shape[0]):
        state, norm = state_of(in_ref, head)
        extra, extra_norm = state_of(first_ref, head)
        for block in range(2):
            if block == 1:
                state, norm = state + extra, norm + extra_norm
            q_feat = features_of(queries[head, block])
            k_feat = features_of(keys[head, block])
            scores = jnp.where(causal, dot(q_feat, k_feat, NT), 0.0)
            den = jnp.sum(scores, axis=1, keepdims=True) + jnp.sum(
                q_feat.astype(F32) * norm, axis=1, keepdims=True
            )
            high, low = split(state)
            out = (
                dot(scores.astype(BF), values[head, block], NN)
                + dot(q_feat, high, NN)
                + dot(q_feat, low, NN)
            ) / den
            att_ref[head, block * BLK : (block + 1) * BLK] = out.astype(BF)
            o_ref[head, block] = out
            den_ref[head, block] = jnp.broadcast_to(den, (BLK, DH))


def scaled_body(
    place,
    queries,
    o_ref,
    den_ref,
    grad_ref,
    grad_other,
    g_ref,
    r_ref,
    sum_ref,
    last_ref,
    grads,
):
    me = place[0]
    cols = pl.ds(pl.multiple_of(me * DH, DH), DH)
    for head in range(queries.shape[0]):
        grads[head, me] = grad_ref[head, :, cols]
        grads[head, 1 - me] = grad_other[head, :, cols]
    for head in range(queries.shape[0]):
        sums, norms = [], []
        for block in range(2):
            q_feat = features_of(queries[head, block])
            scaled = grads[head, block].astype(F32) / den_ref[head, block]
            g_ref[head, block] = scaled
            residue = -jnp.sum(scaled * o_ref[head, block], axis=1, keepdims=True)
            r_ref[head, block] = jnp.broadcast_to(residue, (BLK, DH))
            high, low = split(scaled)
            sums.append(dot(q_feat, high, TN) + dot(q_feat, low, TN))
            norms.append(jnp.sum(residue * q_feat.astype(F32), axis=0, keepdims=True))
        put_state(last_ref, head, sums[1], norms[1])
        put_state(sum_ref, head, sums[0] + sums[1], norms[0] + norms[1])


def backward_body(
    place,
    queries,
    keys,
    values,
    in_ref,
    first_ref,
    g_ref,
    r_ref,
    later_ref,
    last_ref,
    keep_ref,
    send_ref,
    held,
):
    me = place[0]
    causal = causal_mask()
    for head in range(keys.shape[0]):
        state0, norm0 = state_of(in_ref, head)
        extra, extra_norm = state_of(first_ref, head)
        grad1, weight1 = state_of(later_ref, head)
        after, after_norm = state_of(last_ref, head)
        states = (state0, state0 + extra)
        norms = (norm0, norm0 + extra_norm)
        grads = (grad1 + after, grad1)
        weights = (weight1 + after_norm, weight1)
        for block in range(2):
            q_raw = queries[head, block].astype(F32)
            k_raw = keys[head, block].astype(F32)
            v_full = values[head, block]
            q_feat, k_feat = feature(q_raw).astype(BF), feature(k_raw).astype(BF)
            scaled, residue = g_ref[head, block], r_ref[head, block]
            g_high, g_low = split(scaled)
            s_high, s_low = split(states[block])
            grad_high, grad_low = split(grads[block])
            scores = jnp.where(causal, dot(q_feat, k_feat, NT), 0.0).astype(BF)
            mixed = jnp.where(causal, dot(g_high, v_full, NT) + residue, 0.0).astype(BF)
            q_grad = (
                dot(mixed, k_feat, NN)
                + (dot(g_high, s_high, NT) + dot(g_high, s_low, NT) + dot(g_low, s_high, NT))
                + residue * norms[block]
            )
            k_grad = (
                dot(mixed, q_feat, TN)
                + (dot(v_full, grad_high, NT) + dot(v_full, grad_low, NT))
                + weights[block]
            )
            v_grad = dot(scores, g_high, TN) + (
                dot(k_feat, grad_high, NN) + dot(k_feat, grad_low, NN)
            )
            held[block, head, 0] = (q_grad * feature_slope(q_raw)).astype(BF)
            held[block, head, 1] = (k_grad * feature_slope(k_raw)).astype(BF)
            held[block, head, 2] = v_grad.astype(BF)
    keep_ref[...] = held[me]
    send_ref[...] = held[1 - me]


def merge_body(place, keep_ref, back_ref, kept_ref, got_ref, q_ref, k_ref, v_ref, w_ref):
    half = kept_ref.shape[1]
    w_ref[:, pl.ds(pl.multiple_of(place[0] * half, DH), half)] = kept_ref[...]
    w_ref[:, pl.ds(pl.multiple_of((1 - place[0]) * half, DH), half)] = got_ref[...]
    for head in range(keep_ref.shape[0]):
        mine = pl.ds(pl.multiple_of((2 * head + place[0]) * DH, DH), DH)
        other = pl.ds(pl.multiple_of((2 * head + 1 - place[0]) * DH, DH), DH)
        for part, ref in enumerate((q_ref, k_ref, v_ref)):
            ref[:, mine] = keep_ref[head, part]
            ref[:, other] = back_ref[head, part]


def weight_body(steps, count, place, mine_ref, other_ref, *refs):
    *og_refs, send_ref, keep_ref, heads = refs
    left = pl.ds(pl.multiple_of(place[0] * DH, DH), DH)
    right = pl.ds(pl.multiple_of((1 - place[0]) * DH, DH), DH)

    @pl.when(pl.program_id(0) == 0)
    def _():
        for ahead in range(count):
            source = lax.rem(place[3] + ahead, count)
            heads[ahead * BLK : (ahead + 1) * BLK, left] = mine_ref[source]
            heads[ahead * BLK : (ahead + 1) * BLK, right] = other_ref[source]

    right_side = jnp.concatenate([ref[...] for ref in og_refs], axis=0)
    part = dot(heads[...], right_side, TN)

    @pl.when(pl.program_id(0) < steps)
    def _():
        send_ref[...] = part

    @pl.when(pl.program_id(0) >= steps)
    def _():
        keep_ref[...] = part


def on_device(nx, ny, nz, queries, keys, values, out_grad, out_weight):
    chips = nx * ny
    tok, width = queries.shape[1:]
    pairs = width // (2 * DH)
    model = out_grad.shape[2]
    half = model // 2
    me = lax.axis_index("c")
    place = jnp.stack([lax.axis_index(name) for name in ("c", "x", "y", "z")]).astype(jnp.int32)
    q_in, k_in, v_in, og = (
        part.reshape(tok, part.shape[2]) for part in (queries, keys, values, out_grad)
    )
    swap = functools.partial(lax.ppermute, axis_name="c", perm=[(0, 1), (1, 0)])
    plane = ("x", "y")

    def from_ahead(piece, axis, size, ahead):
        return lax.ppermute(piece, axis, [((i + ahead) % size, i) for i in range(size)])

    k_other, v_other, q_other = swap(k_in), swap(v_in), swap(q_in)

    def both_ways(up, down):
        return from_ahead(up, "z", nz, 1), from_ahead(down, "z", nz, -1)

    og_1, og_7 = both_ways(og, og)
    og_2, og_6 = both_ways(og_1, og_7)
    og_3, og_5 = both_ways(og_2, og_6)
    low, high = both_ways(og_3[: tok // 2], og_5[tok // 2 :])
    og_all = kept_out(og, og_1, og_2, og_3, low, high, og_5, og_6, og_7)

    heads = 4
    grid = (pairs // heads,)
    lead = lambda j, p: (j, 0, 0)
    lead4 = lambda j, p: (j, 0, 0, 0)
    state_spec = ((2 * heads, ROWS, DH), lead)
    state_out = (*state_spec, (2 * pairs, ROWS, DH), F32)
    pair_spec = ((heads, 2, tok, DH), lead4)
    pair_out = (*pair_spec, (pairs, 2, tok, DH), F32)
    both_out = (*pair_spec, (pairs, 2, tok, DH), BF)
    head_spec = ((tok, 2 * heads * DH), lambda j, p: (0, j))
    whole = lambda *shape: (shape, lambda j, p: (0,) * len(shape))

    keys_all, values_all, local_sum, first = call(
        local_body, grid, [head_spec] * 4, [both_out, both_out, state_out, state_out]
    )(place, *kept_out(k_in, v_in), k_other, v_other)
    keys_all, values_all, first = kept_out(keys_all, values_all, first)

    out_weight = lax.optimization_barrier((out_weight, local_sum))[0]

    def fetched(piece, axis, size):
        return [from_ahead(piece, axis, size, ahead) for ahead in range(1, size)]

    def gathered(piece, fetched_parts, start):
        size = len(fetched_parts) + 1
        whole = jnp.broadcast_to(piece[None], (size, *piece.shape))
        for ahead, part in enumerate(fetched_parts, start=1):
            place = lax.rem(start + ahead, size)
            whole = lax.dynamic_update_index_in_dim(whole, part, place, 0)
        return whole

    row_group = gathered(out_weight, fetched(out_weight, "y", ny), lax.axis_index("y"))
    row_groups = fetched(row_group, "x", nx)

    parts = lax.all_to_all(local_sum, plane, 0, 0, tiled=True)
    earlier = call(
        scan_body,
        (1,),
        [whole(chips, ROWS, DH)],
        [(*whole(chips, ROWS, DH), (chips, ROWS, DH), F32)],
    )(place, parts)[0]
    earlier = lax.all_to_all(earlier, plane, 0, 0, tiled=True)
    queries_all, earlier, attended, outputs, dens = call(
        forward_body,
        grid,
        [head_spec] * 2 + [pair_spec] * 2 + [state_spec] * 2,
        [both_out, state_out]
        + [((heads, 2 * tok, DH), lead, (pairs, 2 * tok, DH), BF), pair_out, pair_out],
    )(place, *kept_out(q_in), q_other, keys_all, values_all, earlier, first)
    row_groups = lax.optimization_barrier((row_groups, attended))[0]
    rows_mine = gathered(row_group, row_groups, lax.axis_index("x")).reshape(chips, 8, model)
    rows_other = swap(rows_mine)
    rows = jnp.where(
        me == 0,
        jnp.stack([rows_mine, rows_other], axis=1),
        jnp.stack([rows_other, rows_mine], axis=1),
    ).reshape(2 * DH, model)
    att_mine = lax.all_to_all(attended, "z", 0, 0, tiled=True)
    att_other = swap(att_mine)

    ahead_of = [*range(nz // 2), *range(nz // 2 + 1, nz)]
    early = [part for part in og_all if part.shape[0] == tok]
    grads_shape = (nz, tok, 2 * DH)
    attn_grad = call(
        functools.partial(attn_grad_body, nz, ahead_of),
        (1,),
        [(None, None, pl.ANY)] * len(early) + [whole(2 * DH, model)],
        [(*whole(*grads_shape), grads_shape, BF)],
        [
            pltpu.VMEM((len(early) * tok, model), BF),
            pltpu.SemaphoreType.DMA((len(early),)),
        ],
    )(place, *early, rows)[0]
    attn_grad = call(
        last_grad_body,
        (1,),
        [whole(tok // 2, model)] * 2 + [whole(2 * DH, model), (None, None, pl.ANY)],
        [
            (
                (1, tok, 2 * DH),
                lambda j, p: (lax.rem(p[3] + nz // 2, nz), 0, 0),
                grads_shape,
                BF,
            )
        ],
        aliases={4: 0},
    )(place, *kept_out(low, high), rows, *kept_out(attn_grad))[0]
    attn_grad, att_mine = lax.optimization_barrier((attn_grad, att_mine))
    grad_mine = lax.all_to_all(attn_grad, "z", 0, 0, tiled=True)

    steps = 2
    cols = half // steps
    att_spec = ((nz, tok, DH), lambda j, p: (0, p[0], 0))
    og_col = lambda j, p: (0, jnp.where(j < steps, 1 - p[0], p[0]) * steps + lax.rem(j, steps))
    moved, kept = call(
        functools.partial(weight_body, steps, nz),
        (2 * steps,),
        [att_spec] * 2 + [((part.shape[0], cols), og_col) for part in og_all],
        [
            ((2 * DH, cols), lambda j, p: (0, jnp.minimum(j, steps - 1)), (2 * DH, half), F32),
            ((2 * DH, cols), lambda j, p: (0, jnp.maximum(j - steps, 0)), (2 * DH, half), F32),
        ],
        [pltpu.VMEM((nz * tok, 2 * DH), BF)],
    )(place, att_mine, att_other, *og_all)
    grad_mine, moved, kept = lax.optimization_barrier((grad_mine, moved, kept))
    grad_other = swap(grad_mine)
    got = swap(moved)

    grad_spec = ((heads, tok, 2 * DH), lead)
    scaled, residue, grad_sum, last = call(
        scaled_body,
        grid,
        [pair_spec] * 3 + [grad_spec] * 2,
        [pair_out, pair_out, state_out, state_out],
        [pltpu.VMEM((heads, 2, tok, DH), BF)],
    )(
        place,
        *kept_out(queries_all, outputs, dens),
        *(grad_mine, grad_other),
    )
    parts = lax.all_to_all(grad_sum, plane, 0, 0, tiled=True)
    later = call(
        back_scan_body,
        (1,),
        [whole(chips, ROWS, DH)],
        [(*whole(chips, ROWS, DH), (chips, ROWS, DH), F32)],
    )(place, parts)[0]
    later = lax.all_to_all(later, plane, 0, 0, tiled=True)
    shares = (kept + got).astype(BF).reshape(chips, 2 * DH // chips, half)
    later, shares = lax.optimization_barrier((later, shares))
    shares = lax.all_to_all(shares, plane, 0, 0, tiled=True)
    grad_out = ((heads, 3, tok, DH), lead4, (pairs, 3, tok, DH), BF)
    keep, send = call(
        backward_body,
        grid,
        [pair_spec] * 3
        + [state_spec, state_spec, pair_spec, pair_spec, state_spec, state_spec],
        [grad_out] * 2,
        [pltpu.VMEM((2, heads, 3, tok, DH), BF)],
    )(
        place,
        *kept_out(queries_all, keys_all, values_all, earlier, first, scaled, residue),
        later,
        *kept_out(last),
    )
    send, shares = lax.optimization_barrier((send, shares))
    back = swap(send)
    weight_kept, weight_moved = call(
        total_body,
        (1,),
        [whole(*shares.shape)],
        [(*whole(8, half), (8, half), F32)] * 2,
    )(place, shares)
    weight_got = swap(weight_moved)
    *grads, weight_grad = call(
        merge_body,
        (1,),
        [whole(pairs, 3, tok, DH)] * 2 + [whole(8, half)] * 2,
        [(*whole(tok, width), (tok, width), BF)] * 3
        + [(*whole(8, model), (8, model), F32)],
    )(place, *kept_out(keep), back, weight_kept, weight_got)
    return (*(grad.reshape(1, tok, width) for grad in grads), weight_grad)


def solution(mesh):
    nz, nx, ny = mesh.shape["dp"], 4, mesh.shape["seq"] // 8
    grid = Mesh(mesh.devices.reshape(nz, nx, ny, 2), ("z", "x", "y", "c"))
    tokens = P("z", ("x", "y", "c"), None)
    weights = P(("z", "x", "y", "c"), None)
    return jax.shard_map(
        functools.partial(on_device, nx, ny, nz),
        mesh=grid,
        in_specs=(tokens, tokens, tokens, tokens, weights),
        out_specs=(tokens, tokens, tokens, weights),
        check_vma=False,
    )
```
